256 devices in a mesh: cell: 8 (over z_lo, x), conf: 32 (over y, z_hi, core).
Axes of the slice: x: 4, y: 4, z: 8 (z_hi: 4, z_lo: 2; z = z_hi * 2 + z_lo), core: 2. Of those that a mesh axis runs over, the one named last changes fastest.
Arguments:
- density: float32 [32, 32, 32, 4096], P('conf', None, None, 'cell'), may hold values from 0 to 8, as said below
- velocity: float32 [2, 16, 256], P(None, 'cell'), may hold values from -12 to 12
- short_stress: float32 [3, 4096], P(None, ('cell', 'conf')), may hold values from -6 to 6
Outputs:
- density_next: float32 [32, 32, 32, 4096], P('conf', None, None, 'cell')
- short_next: float32 [3, 4096], P(None, ('cell', 'conf'))
- total_stress: float32 [3, 4096], P(None, ('cell', 'conf'))
The draws below stay inside these ranges and needn't reach their ends.
Inputs may be any that keep to these rules, and one draw needn't show every extreme that they name: Each cell's configuration density is positive.
All inputs are finite; a program needn't handle non-finite values.
Results may differ from the reference program's by a relative error of at most 0.00012.
Values sent between devices are 32-bit elements; how exact they have to be, the bound alone decides.
A program may use at most 192 MiB of HBM per device.

```python
import jax
import jax.numpy as jnp
from jax import lax

Q = 32
COLS = 256
STEPS = 2
ROWS = 16
CELLS = 4096


def draw_density(key, part):
    key = jax.random.fold_in(key, 11)
    scale_key, rough_key = jax.random.split(key)
    level = jnp.exp(jax.random.uniform(scale_key, (CELLS,), jnp.float32, jnp.log(0.3), jnp.log(3.0)))
    rough = jax.random.uniform(rough_key, (Q, Q, Q, CELLS), jnp.float32, -1.0, 1.0)
    return level * (1.0 + 0.5 * rough)


def levels(rng, extent, pieces, least, largest):
    level, own = 1.0, jax.random.fold_in(rng, 6)
    for position, blocks in pieces:
        steps = jnp.exp(jax.random.uniform(jax.random.fold_in(own, position), (blocks,), jnp.float32, least / len(pieces), largest / len(pieces)))
        level = level * jnp.repeat(steps, extent[position] // blocks).reshape([-1 if axis == position else 1 for axis in range(len(extent))])
    return level


def scatter_about(own_key, dims, width, bound, pieces=(), held_as=jnp.bfloat16):
    values = width * jax.random.normal(own_key, dims, jnp.float32)
    if pieces:
        values = values * levels(own_key, dims, pieces, -0.22, 0.18)
    return jnp.clip(values, -bound, bound).astype(held_as)


def setup_inputs(seed: int = 0) -> dict:
    key_list = jax.random.split(jax.random.key(seed), 4)
    return {
        "density": draw_density(jax.random.fold_in(key_list[3], 71), 0),
        "velocity": scatter_about(key_list[1], (2, ROWS, COLS), 3.0, 12.0, ((1, 8),), jnp.float32),
        "short_stress": scatter_about(key_list[2], (3, CELLS), 1.0, 6.0, ((1, 256),), jnp.float32),
    }


half_extent = 3.0
fene_limit = 50.0
diffusion = 0.5
time_step = 0.001
polymer_eta = 1.0
solvent_eta = 0.5
short_relax = 0.01


def spectral_matrix(points):
    offsets = jnp.arange(points)[:, None] - jnp.arange(points)[None, :]
    phase_angle = offsets.astype(jnp.float32) * (jnp.pi / points)
    sine_value = jnp.where(offsets == 0, jnp.float32(1.0), jnp.sin(phase_angle))
    parity = jnp.where(offsets % 2 == 0, 1.0, -1.0).astype(jnp.float32)
    entries = parity * jnp.cos(phase_angle) / sine_value * (jnp.pi / (2.0 * half_extent))
    return jnp.where(offsets == 0, jnp.float32(0.0), entries)


def grid_points(points):
    return -half_extent + (jnp.arange(points, dtype=jnp.float32) + 0.5) * (2.0 * half_extent / points)


def derive(values, which_axis, diff_matrix):
    patterns = ("jk,kabc->jabc", "jk,akbc->ajbc", "jk,abkc->abjc")
    return jnp.einsum(patterns[which_axis], diff_matrix, values, precision=lax.Precision.HIGHEST)


def drifts(coord_first, coords, gradient):
    coord_a = coord_first[:, None, None, None]
    coord_b = coords[None, :, None, None]
    coord_c = coords[None, None, :, None]
    spring = 1.0 / (1.0 - (coord_a * coord_a + coord_b * coord_b + coord_c * coord_c) / fene_limit)
    drift_a = gradient[0] * coord_a + gradient[1] * coord_b - diffusion * spring * coord_a
    drift_b = gradient[2] * coord_a + gradient[3] * coord_b - diffusion * spring * coord_b
    drift_c = -diffusion * spring * coord_c
    return drift_a, drift_b, drift_c


def advance(density, gradient, diff_matrix, coords):
    drift_set = drifts(coords, coords, gradient)
    change = jnp.zeros_like(density)
    for which_axis in range(3):
        flux_term = drift_set[which_axis] * density - diffusion * derive(density, which_axis, diff_matrix)
        change = change + derive(flux_term, which_axis, diff_matrix)
    return density - time_step * change


def moment_weights(coord_first, coords):
    points = coords.shape[0]
    coord_a = coord_first[:, None, None]
    coord_b = coords[None, :, None]
    coord_c = coords[None, None, :]
    spring = 1.0 / (1.0 - (coord_a * coord_a + coord_b * coord_b + coord_c * coord_c) / fene_limit)
    scale = 1.0 / float(points ** 3)
    stacked = jnp.stack([coord_a * coord_a * spring, coord_a * coord_b * spring, coord_b * coord_b * spring, jnp.ones_like(spring)])
    return (stacked * scale).reshape(4, -1)


def relax(stress, gradient):
    stress_xx, stress_xy, stress_yy = stress[0], stress[1], stress[2]
    for turn_index in range(STEPS):
        next_xx = stress_xx + time_step * (2.0 * (gradient[0] * stress_xx + gradient[1] * stress_xy) - (stress_xx - 2.0 * solvent_eta * gradient[0]) / short_relax)
        next_xy = stress_xy + time_step * (gradient[0] * stress_xy + gradient[1] * stress_yy + gradient[2] * stress_xx + gradient[3] * stress_xy - (stress_xy - solvent_eta * (gradient[1] + gradient[2])) / short_relax)
        next_yy = stress_yy + time_step * (2.0 * (gradient[2] * stress_xy + gradient[3] * stress_yy) - (stress_yy - 2.0 * solvent_eta * gradient[3]) / short_relax)
        stress_xx, stress_xy, stress_yy = next_xx, next_xy, next_yy
    return jnp.stack([stress_xx, stress_xy, stress_yy])


def combine_stress(moments, short_next):
    polymer = jnp.stack([polymer_eta * (moments[0] - moments[3]), polymer_eta * moments[1], polymer_eta * (moments[2] - moments[3])])
    return polymer + short_next


def reference(density, velocity, short_stress):
    points = density.shape[0]
    rows_total = velocity.shape[1]
    row_cells = velocity.shape[2]
    diff_matrix = spectral_matrix(points)
    coords = grid_points(points)
    grad_x = (jnp.roll(velocity, -1, 2) - jnp.roll(velocity, 1, 2)) * 0.5
    grad_y = (jnp.roll(velocity, -1, 1) - jnp.roll(velocity, 1, 1)) * 0.5
    gradient = jnp.stack([grad_x[0], grad_y[0], grad_x[1], grad_y[1]])
    weights = moment_weights(coords, coords)
    blocks = jnp.moveaxis(density.reshape(points, points, points, rows_total, row_cells), 3, 0)
    grad_blocks = jnp.moveaxis(gradient, 1, 0)

    def one_row(row_inputs):
        values, grads = row_inputs
        for turn_index in range(STEPS):
            values = advance(values, grads, diff_matrix, coords)
        moments = jnp.dot(weights, values.reshape(points ** 3, row_cells), precision=lax.Precision.HIGHEST, preferred_element_type=jnp.float32)
        return values, moments

    advanced, moment_rows = lax.map(one_row, (blocks, grad_blocks))
    density_next = jnp.moveaxis(advanced, 0, 3).reshape(points, points, points, rows_total * row_cells)
    moments = jnp.moveaxis(moment_rows, 0, 1).reshape(4, rows_total * row_cells)
    short_next = relax(short_stress, gradient.reshape(4, rows_total * row_cells))
    return density_next, short_next, combine_stress(moments, short_next)
```

```python
import functools

import jax
import jax.numpy as jnp
import ml_dtypes
import numpy as np
from jax import lax
from jax.experimental import pallas as pl
from jax.experimental.pallas import tpu as pltpu
from jax.sharding import PartitionSpec as P

STEPS = 2
half_extent = 3.0
fene_limit = 50.0
diffusion = 0.5
time_step = 0.001
polymer_eta = 1.0
solvent_eta = 0.5
short_relax = 0.01

MESH = pl.DeviceIdType.MESH
Q = 32
GROUP = 32
OWN = 16
PART = 8
PARTS = 2
LANES = Q * PART
CELLS = GROUP * OWN


def operators():
    offsets = np.arange(Q)[:, None] - np.arange(Q)[None, :]
    angle = offsets * (np.pi / Q)
    sine = np.where(offsets == 0, 1.0, np.sin(angle))
    first = np.where(offsets % 2 == 0, 1.0, -1.0) * np.cos(angle) / sine * (np.pi / (2 * half_extent))
    first = np.where(offsets == 0, 0.0, first)
    pair = (-time_step * first, time_step * diffusion * (first @ first))
    eye = np.eye(8)

    def parts(matrix):
        high = matrix.astype(np.float32).astype(ml_dtypes.bfloat16)
        low = (matrix - high.astype(np.float64)).astype(np.float32).astype(ml_dtypes.bfloat16)
        return [high, high, low]

    along_a = np.concatenate([q for m in pair for q in parts(np.kron(m, eye))], axis=1)
    along_b = np.concatenate([q for m in pair for q in parts(np.kron(eye, m))], axis=1)
    along_c = np.concatenate([q for m in pair for q in parts(np.kron(m.T, eye))], axis=0)
    return along_a, along_b, along_c


def springs():
    coords = -half_extent + (np.arange(Q) + 0.5) * (2 * half_extent / Q)
    squares = coords * coords
    total = squares[:, None, None] + squares[None, :, None] + squares[None, None, :]
    spring = 1.0 / (1.0 - total / fene_limit)
    return np.repeat(spring, PART, axis=2).astype(np.float32)


def coord(index):
    return -half_extent + (index.astype(jnp.float32) + 0.5) * (2.0 * half_extent / Q)


def split(value):
    high = value.astype(jnp.bfloat16)
    low = (value - high.astype(jnp.float32)).astype(jnp.bfloat16)
    return [high, low, high]


def exchange_lanes(values):
    lane = lax.broadcasted_iota(jnp.int32, (8, 128), 1)
    values = list(values)
    for bit in (1, 2, 4, 8):
        upper = (lane & (8 * bit)) != 0
        shift = 8 * bit
        for i in range(16):
            if i & bit:
                continue
            one, two = values[i], values[i | bit]
            values[i] = jnp.where(upper, pltpu.roll(two, shift, 1), one)
            values[i | bit] = jnp.where(upper, two, pltpu.roll(one, 128 - shift, 1))
    return values


def exact_dot(one, two):
    return jnp.dot(one, two, precision=lax.Precision.HIGHEST, preferred_element_type=jnp.float32)


def relax(stress, gradient):
    stress_xx, stress_xy, stress_yy = stress
    for _ in range(STEPS):
        next_xx = stress_xx + time_step * (
            2.0 * (gradient[0] * stress_xx + gradient[1] * stress_xy)
            - (stress_xx - 2.0 * solvent_eta * gradient[0]) / short_relax
        )
        next_xy = stress_xy + time_step * (
            gradient[0] * stress_xy
            + gradient[1] * stress_yy
            + gradient[2] * stress_xx
            + gradient[3] * stress_xy
            - (stress_xy - solvent_eta * (gradient[1] + gradient[2])) / short_relax
        )
        next_yy = stress_yy + time_step * (
            2.0 * (gradient[2] * stress_xy + gradient[3] * stress_yy)
            - (stress_yy - 2.0 * solvent_eta * gradient[3]) / short_relax
        )
        stress_xx, stress_xy, stress_yy = next_xx, next_xy, next_yy
    return stress_xx, stress_xy, stress_yy


def kernel(
    density_hbm, velocity, short, wa_hbm, wb_hbm, wc_hbm, spring_hbm,
    out_hbm, short_out, total_out,
    density, out, packed, grid, back, change, spring, wa, wb, wc, halo, lanes, sums, moments,
    in_send, in_recv, out_send, out_recv, load_sem, halo_send, halo_recv, read_sem, write_sem,
):
    me = lax.axis_index("conf")
    my_y, my_z, my_c = me // 8, (me // 2) % 4, me % 2
    brick = lax.axis_index("cell")
    bricks = lax.axis_size("cell")
    above, below = lax.rem(brick + bricks - 1, bricks), lax.rem(brick + 1, bricks)

    reads = [
        pltpu.make_async_copy(density_hbm.at[:, pl.ds(i * 128, 128)], density.at[i], read_sem.at[i])
        for i in range(4)
    ]
    for read in reads:
        read.start()
    barrier = pltpu.get_barrier_semaphore()

    def greet(turn, carry):
        pl.semaphore_signal(barrier, inc=1, device_id={"conf": lax.rem(me + turn, GROUP)}, device_id_type=MESH)
        return carry

    lax.fori_loop(1, GROUP, greet, 0)
    for other in (above, below):
        pl.semaphore_signal(barrier, inc=1, device_id={"cell": other}, device_id_type=MESH)

    loads = [
        pltpu.make_async_copy(source, target, load_sem.at[i])
        for i, (source, target) in enumerate(((wa_hbm, wa), (wb_hbm, wb), (wc_hbm, wc), (spring_hbm, spring)))
    ]
    for load in loads:
        load.start()

    def peer(dy, turn):
        dz, dc = turn // 2, turn % 2
        return lax.rem(my_y + dy, 4) * 8 + lax.rem(my_z + dz, 4) * 2 + lax.rem(my_c + dc, 2)

    def pack(block):
        def piece(turn, carry):
            tile, half = turn // 2, turn % 2
            values = [
                density[block, pl.ds(tile * 256 + half * 16 + i, 8, stride=Q), :] for i in range(16)
            ]
            values = exchange_lanes(values)
            for i in range(16):
                packed[
                    i % 2, block * 8 + i // 2, pl.ds(pl.multiple_of(tile * 8, 8), 8),
                    pl.ds(pl.multiple_of(half * 128, 128), 128),
                ] = values[i]
            return carry

        lax.fori_loop(0, 8, piece, 0)

    def send_in(part, dy):
        def one(turn, carry):
            target = peer(dy, turn)
            pltpu.make_async_remote_copy(
                packed.at[part, target], grid.at[part, me], in_send.at[part], in_recv.at[part],
                device_id={"conf": target}, device_id_type=MESH,
            ).start()
            return carry

        lax.fori_loop(jnp.where(dy == 0, 1, 0), 8, one, 0)

    for read in reads:
        read.wait()
    pack(my_y)
    pl.semaphore_wait(barrier, GROUP + 1)
    to_above = pltpu.make_async_remote_copy(
        velocity, halo.at[1], halo_send.at[0], halo_recv.at[1], device_id={"cell": above}, device_id_type=MESH
    )
    to_below = pltpu.make_async_remote_copy(
        velocity, halo.at[0], halo_send.at[1], halo_recv.at[0], device_id={"cell": below}, device_id_type=MESH
    )
    to_above.start()
    to_below.start()
    send_in(0, jnp.int32(0))

    def pack_and_send(dy, carry):
        pack(lax.rem(my_y + dy, 4))
        send_in(0, dy)
        return carry

    lax.fori_loop(1, 4, pack_and_send, 0)

    def send_late(dy, carry):
        send_in(1, dy)
        return carry

    lax.fori_loop(0, 4, send_late, 0)
    for part in range(PARTS):
        pltpu.make_async_copy(packed.at[part, me], grid.at[part, me], in_recv.at[part]).start()

    to_above.wait()
    to_below.wait()
    rows = velocity.shape[1]
    first_row = me < GROUP // 2
    picked = []
    for i in range(2):
        here = velocity[i]
        along = (pltpu.roll(here, here.shape[1] - 1, 1) - pltpu.roll(here, 1, 1)) * 0.5
        before, after = halo[0, i], halo[1, i]
        picked.append(jnp.where(first_row, along[0:1], along[1:2]))
        down_first = (here[1:2] - before[rows - 1 : rows]) * 0.5
        down_last = (after[0:1] - here[rows - 2 : rows - 1]) * 0.5
        picked.append(jnp.where(first_row, down_first, down_last))
    picked = jnp.concatenate(picked + [jnp.zeros((4, picked[0].shape[1]), jnp.float32)], axis=0)
    width = picked.shape[1]
    offset = lax.rem(me, GROUP // 2) * OWN
    source = lax.broadcasted_iota(jnp.int32, (width, LANES), 0) - offset
    lane = lax.broadcasted_iota(jnp.int32, (width, LANES), 1)
    for part in range(PARTS):
        choose = (source == (lane & (PART - 1)) + part * PART).astype(jnp.float32)
        lanes[part] = exact_dot(picked, choose)
    own_source = lax.broadcasted_iota(jnp.int32, (width, 128), 0) - offset
    own_lane = lax.broadcasted_iota(jnp.int32, (width, 128), 1)
    own = exact_dot(picked, ((own_source == own_lane) & (own_lane < OWN)).astype(jnp.float32))
    relaxed = relax(
        tuple(short[i : i + 1, :] for i in range(3)), tuple(own[i : i + 1, :OWN] for i in range(4))
    )
    for i in range(3):
        short_out[i : i + 1, :] = relaxed[i]
    moments[...] = jnp.zeros_like(moments)
    for load in loads:
        load.wait()

    coord_c = coord(lax.broadcasted_iota(jnp.int32, (1, 1, LANES), 2) // PART)
    coord_all = coord(lax.broadcasted_iota(jnp.int32, (1, Q, 1), 1))

    def advance(part, last):
        k11, k12, k21, k22 = (lanes[part, i : i + 1, :].reshape(1, 1, LANES) for i in range(4))

        def first_direction(tile, carry):
            window = pl.ds(pl.multiple_of(tile * 8, 8), 8)
            value = grid[part, :, window, :]
            coord_a = coord(lax.broadcasted_iota(jnp.int32, (Q, 1, 1), 0))
            coord_b = coord(lax.broadcasted_iota(jnp.int32, (1, 8, 1), 1) + tile * 8)
            drift = (k11 - diffusion * spring[:, window, :]) * coord_a + k12 * coord_b
            moved = (drift * value).reshape(Q * 8, LANES)
            terms = jnp.concatenate(split(moved) + split(value.reshape(Q * 8, LANES)), axis=0)
            result = jnp.dot(wa[...], terms, preferred_element_type=jnp.float32)
            change[:, window, :] = result.reshape(Q, 8, LANES)
            return carry

        lax.fori_loop(0, 4, first_direction, 0)

        def other_directions(tile, carry):
            window = pl.ds(tile * 8, 8)
            value = grid[part, window]
            stiff = spring[window]
            coord_a = coord(lax.broadcasted_iota(jnp.int32, (8, 1, 1), 0) + tile * 8)
            pull = diffusion * stiff
            drift_b = k21 * coord_a + (k22 - pull) * coord_all
            moved_b = (drift_b * value).reshape(8 * Q, LANES)
            moved_c = (-pull * coord_c * value).reshape(8 * Q, LANES)
            plain = split(value.reshape(8 * Q, LANES))
            terms_b = jnp.concatenate(split(moved_b) + plain, axis=0)
            part_b = jnp.dot(wb[...], terms_b, preferred_element_type=jnp.float32)
            terms_c = jnp.concatenate(split(moved_c) + plain, axis=1)
            part_c = jnp.dot(terms_c, wc[...], preferred_element_type=jnp.float32)
            value = value + (change[window] + (part_b + part_c).reshape(8, Q, LANES))
            grid[part, window] = value
            if last:
                weighted = stiff * value
                sums[0] += jnp.sum(weighted, axis=0)
                weighted = weighted * coord_a
                sums[1] += jnp.sum(weighted, axis=0)
                sums[2] += jnp.sum(weighted * coord_a, axis=0)
                sums[3] += jnp.sum(value, axis=0)
            return carry

        lax.fori_loop(0, 4, other_directions, 0)

    def whole(part, carry):
        pltpu.make_async_copy(grid.at[part], grid.at[part], in_recv.at[part]).wait()
        sums[...] = jnp.zeros_like(sums)
        for turn in range(STEPS):
            advance(part, turn == STEPS - 1)

        def send_out(turn, inner):
            target = peer(turn // 8, lax.rem(turn, 8))
            pltpu.make_async_remote_copy(
                grid.at[part, target], back.at[part, me], out_send.at[part], out_recv.at[part],
                device_id={"conf": target}, device_id_type=MESH,
            ).start()
            return inner

        lax.fori_loop(1, GROUP, send_out, 0)
        pltpu.make_async_copy(grid.at[part, me], back.at[part, me], out_recv.at[part]).start()
        column = coord(lax.broadcasted_iota(jnp.int32, (Q, 1), 0))
        scale = 1.0 / float(Q**3)
        stacked = jnp.concatenate(
            [
                jnp.sum(sums[2], axis=0, keepdims=True),
                jnp.sum(sums[1] * column, axis=0, keepdims=True),
                jnp.sum(sums[0] * (column * column), axis=0, keepdims=True),
                jnp.sum(sums[3], axis=0, keepdims=True),
                jnp.zeros((4, LANES), jnp.float32),
            ],
            axis=0,
        )
        fold_row = lax.broadcasted_iota(jnp.int32, (LANES, 128), 0) & (PART - 1)
        fold_lane = lax.broadcasted_iota(jnp.int32, (LANES, 128), 1) - part * PART
        moments[...] += exact_dot(stacked * scale, (fold_row == fold_lane).astype(jnp.float32))
        return carry

    lax.fori_loop(0, PARTS, whole, 0)

    total = moments[...]
    for i, polymer in enumerate(
        (
            polymer_eta * (total[0:1] - total[3:4]),
            polymer_eta * total[1:2],
            polymer_eta * (total[2:3] - total[3:4]),
        )
    ):
        total_out[i : i + 1, :] = polymer[:, :OWN] + short_out[i : i + 1, :]

    for part in range(PARTS):
        pltpu.make_async_copy(back.at[part], back.at[part], out_recv.at[part]).wait()

    def unpack(block, carry):
        def piece(turn, inner):
            tile, half = turn // 2, turn % 2
            values = [
                back[
                    i % 2, block * 8 + i // 2, pl.ds(pl.multiple_of(tile * 8, 8), 8),
                    pl.ds(pl.multiple_of(half * 128, 128), 128),
                ]
                for i in range(16)
            ]
            values = exchange_lanes(values)
            for i in range(16):
                out[block, pl.ds(tile * 256 + half * 16 + i, 8, stride=Q), :] = values[i]
            return inner

        lax.fori_loop(0, 8, piece, 0)
        pltpu.make_async_copy(
            out.at[block], out_hbm.at[:, pl.ds(pl.multiple_of(block * 128, 128), 128)], write_sem.at[block]
        ).start()
        return carry

    lax.fori_loop(0, 4, unpack, 0)
    for i in range(4):
        pltpu.make_async_copy(out.at[i], out_hbm.at[:, pl.ds(i * 128, 128)], write_sem.at[i]).wait()
    others = pl.ds(0, GROUP - 1)
    for part in range(PARTS):
        pltpu.make_async_copy(packed.at[part, others], packed.at[part, others], in_send.at[part]).wait()
        pltpu.make_async_copy(grid.at[part, others], grid.at[part, others], out_send.at[part]).wait()


def on_device(density, velocity, short_stress):
    along_a, along_b, along_c = operators()
    spring = springs()
    vmem = pl.BlockSpec(memory_space=pltpu.VMEM)
    anywhere = pl.BlockSpec(memory_space=pl.ANY)
    blocks = (PARTS, GROUP, Q, LANES)
    dma = pltpu.SemaphoreType.DMA
    result, short_next, total_stress = pl.pallas_call(
        kernel,
        name="fokker_planck",
        out_shape=(
            jax.ShapeDtypeStruct((Q * Q, CELLS), jnp.float32),
            jax.ShapeDtypeStruct((3, OWN), jnp.float32),
            jax.ShapeDtypeStruct((3, OWN), jnp.float32),
        ),
        in_specs=[anywhere, vmem, vmem, anywhere, anywhere, anywhere, anywhere],
        out_specs=(anywhere, vmem, vmem),
        scratch_shapes=[
            pltpu.VMEM((4, Q * Q, 128), jnp.float32),
            pltpu.VMEM((4, Q * Q, 128), jnp.float32),
            pltpu.VMEM(blocks, jnp.float32),
            pltpu.VMEM(blocks, jnp.float32),
            pltpu.VMEM(blocks, jnp.float32),
            pltpu.VMEM((Q, Q, LANES), jnp.float32),
            pltpu.VMEM(spring.shape, jnp.float32),
            pltpu.VMEM(along_a.shape, jnp.bfloat16),
            pltpu.VMEM(along_b.shape, jnp.bfloat16),
            pltpu.VMEM(along_c.shape, jnp.bfloat16),
            pltpu.VMEM((2,) + velocity.shape, jnp.float32),
            pltpu.VMEM((PARTS, 8, LANES), jnp.float32),
            pltpu.VMEM((4, Q, LANES), jnp.float32),
            pltpu.VMEM((8, 128), jnp.float32),
            dma((PARTS,)),
            dma((PARTS,)),
            dma((PARTS,)),
            dma((PARTS,)),
            dma((4,)),
            dma((2,)),
            dma((2,)),
            dma((4,)),
            dma((4,)),
        ],
        compiler_params=pltpu.CompilerParams(
            collective_id=0, has_side_effects=True, vmem_limit_bytes=48 * 1024 * 1024
        ),
    )(
        density.reshape(Q * Q, CELLS),
        velocity,
        short_stress,
        along_a,
        along_b,
        along_c,
        spring,
    )
    return result.reshape(density.shape), short_next, total_stress


def solution(mesh):
    return jax.shard_map(
        on_device,
        mesh=mesh,
        in_specs=(P("conf", None, None, "cell"), P(None, "cell", None), P(None, ("cell", "conf"))),
        out_specs=(
            P("conf", None, None, "cell"),
            P(None, ("cell", "conf")),
            P(None, ("cell", "conf")),
        ),
        check_vma=False,
    )
```

```python
import functools

import jax
import jax.numpy as jnp
import numpy as np
from jax import lax
from jax.experimental import pallas as pl
from jax.experimental.pallas import tpu as pltpu
from jax.sharding import PartitionSpec as P

STEPS = 2
half_extent = 3.0
fene_limit = 50.0
diffusion = 0.5
time_step = 0.001
polymer_eta = 1.0
solvent_eta = 0.5
short_relax = 0.01

MESH = pl.DeviceIdType.MESH
Q = 32
GROUP = 32
OWN = 16
PART = 8
PARTS = 2
LANES = Q * PART
CELLS = GROUP * OWN
TALL = 32
VMEM_LIMIT = 61 * 1024 * 1024


def stencils():
    offsets = np.arange(Q)[:, None] - np.arange(Q)[None, :]
    angle = offsets * (np.pi / Q)
    sine = np.where(offsets == 0, 1.0, np.sin(angle))
    first = np.where(offsets % 2 == 0, 1.0, -1.0) * np.cos(angle) / sine * (np.pi / (2 * half_extent))
    first = np.where(offsets == 0, 0.0, first)
    return (-time_step * first)[:, 0], (time_step * diffusion * (first @ first))[:, 0]


def build_operators(wa, wb, wc):
    first, second = stencils()
    size = 8 * Q
    row = lax.broadcasted_iota(jnp.int32, (size, size), 0)
    column = lax.broadcasted_iota(jnp.int32, (size, size), 1)

    def circulant(offset, inside):
        key = jnp.where(inside, offset & (Q - 1), -1)
        one, two = (jnp.zeros((size, size), jnp.float32) for _ in range(2))
        for i in range(Q):
            here = key == i
            one = jnp.where(here, jnp.float32(first[i]), one)
            two = jnp.where(here, jnp.float32(second[i]), two)
        return one, two

    def store(ref, matrix, at, by_row):
        high, low, again = split(matrix)
        for i, value in enumerate((high, again, low)):
            place = pl.ds((at + i) * size, size)
            if by_row:
                ref[place, :] = value
            else:
                ref[:, place] = value

    one, two = circulant((row >> 3) - (column >> 3), (row & 7) == (column & 7))
    store(wa, one, 0, False)
    store(wa, two, 3, False)
    store(wc, -one, 0, True)
    store(wc, two, 3, True)
    one, two = circulant(row - column, (row >> 5) == (column >> 5))
    store(wb, one, 0, False)
    store(wb, two, 3, False)


def coord(index):
    return -half_extent + (index.astype(jnp.float32) + 0.5) * (2.0 * half_extent / Q)


def split(value):
    high = value.astype(jnp.bfloat16)
    low = (value - high.astype(jnp.float32)).astype(jnp.bfloat16)
    return [high, low, high]


def exchange_lanes(values):
    lane = lax.broadcasted_iota(jnp.int32, values[0].shape, 1)
    values = list(values)
    for bit in (1, 2, 4, 8):
        upper = (lane & (8 * bit)) != 0
        shift = 8 * bit
        for i in range(16):
            if i & bit:
                continue
            one, two = values[i], values[i | bit]
            mixed = jnp.where(upper, one, two)
            if shift == 64:
                mixed = pltpu.roll(mixed, 64, 1)
            else:
                mixed = jnp.take_along_axis(mixed, lane ^ shift, axis=1, mode="promise_in_bounds")
            values[i] = jnp.where(upper, mixed, one)
            values[i | bit] = jnp.where(upper, two, mixed)
    return values


def unpack(arrived, target, block):
    def piece(turn, carry):
        tile, half = turn // 2, turn % 2
        values = [
            arrived[
                block * 16 + i, pl.ds(pl.multiple_of(tile * TALL, TALL), TALL),
                pl.ds(pl.multiple_of(half * 128, 128), 128),
            ]
            for i in range(16)
        ]
        values = exchange_lanes(values)
        for i in range(16):
            target[pl.ds(tile * (TALL * Q) + half * 16 + i, TALL, stride=Q), :] = values[i]
        return carry

    lax.fori_loop(0, 2 * Q // TALL, piece, 0)


def exact_dot(one, two):
    return jnp.dot(one, two, precision=lax.Precision.HIGHEST, preferred_element_type=jnp.float32)


def relax(stress, gradient):
    stress_xx, stress_xy, stress_yy = stress
    for _ in range(STEPS):
        next_xx = stress_xx + time_step * (
            2.0 * (gradient[0] * stress_xx + gradient[1] * stress_xy)
            - (stress_xx - 2.0 * solvent_eta * gradient[0]) / short_relax
        )
        next_xy = stress_xy + time_step * (
            gradient[0] * stress_xy
            + gradient[1] * stress_yy
            + gradient[2] * stress_xx
            + gradient[3] * stress_xy
            - (stress_xy - solvent_eta * (gradient[1] + gradient[2])) / short_relax
        )
        next_yy = stress_yy + time_step * (
            2.0 * (gradient[2] * stress_xy + gradient[3] * stress_yy)
            - (stress_yy - 2.0 * solvent_eta * gradient[3]) / short_relax
        )
        stress_xx, stress_xy, stress_yy = next_xx, next_xy, next_yy
    return stress_xx, stress_xy, stress_yy


def kernel(
    density_hbm, velocity_hbm, short_hbm,
    early_hbm, late, stress,
    density, velocity, short, early, early_back, inbox, packed, grid, change, spring, wa, wb, wc, halo, lanes, sums, moments,
    in_send, in_recv, out_send, out_recv, load_sem, halo_send, halo_recv, read_sem,
    note_send, note_recv, write_sem,
):
    me = lax.axis_index("conf")
    my_y, my_z, my_c = me // 8, (me // 2) % 4, me % 2
    brick = lax.axis_index("cell")
    bricks = lax.axis_size("cell")
    above, below = lax.rem(brick + bricks - 1, bricks), lax.rem(brick + 1, bricks)

    reads = [
        pltpu.make_async_copy(
            density_hbm.at[:, pl.ds(pl.multiple_of(block * 128, 128), 128)], density.at[block], read_sem.at[i]
        )
        for i, block in enumerate([2 * (i // 2) + lax.rem(my_y // 2 + i, 2) for i in range(4)])
    ]
    for read in reads:
        read.start()
    barrier = pltpu.get_barrier_semaphore()

    def greet(turn, carry):
        pl.semaphore_signal(barrier, inc=1, device_id={"conf": lax.rem(me + turn, GROUP)}, device_id_type=MESH)
        return carry

    lax.fori_loop(1, GROUP, greet, 0)
    for other in (above, below):
        pl.semaphore_signal(barrier, inc=1, device_id={"cell": other}, device_id_type=MESH)

    loads = [
        pltpu.make_async_copy(source, target, load_sem.at[i])
        for i, (source, target) in enumerate(
            ((velocity_hbm, velocity), (short_hbm, short))
        )
    ]
    for load in loads:
        load.start()

    def side(turn):
        return lax.rem(my_y // 2 + turn, 2)

    def peer(half, turn):
        y = 2 * side(half) + lax.rem(my_y + turn // 8, 2)
        z = lax.rem(my_z + lax.rem(turn, 8) // 2, 4)
        return y * 8 + z * 2 + lax.rem(my_c + turn, 2)

    def pack(part, half):
        first = side(half)
        block = part * 2 + first

        def piece(turn, carry):
            tile, half = turn // 2, turn % 2
            values = [
                density[block, pl.ds(tile * (TALL * Q) + half * 16 + i, TALL, stride=Q), :] for i in range(16)
            ]
            values = exchange_lanes(values)
            for i in range(16):
                packed[
                    part, first * 16 + i, pl.ds(pl.multiple_of(tile * TALL, TALL), TALL),
                    pl.ds(pl.multiple_of(half * 128, 128), 128),
                ] = values[i]
            return carry

        lax.fori_loop(0, 2 * Q // TALL, piece, 0)

    def send_in(part, half):
        def one(turn, carry):
            target = peer(half, turn)
            pltpu.make_async_remote_copy(
                packed.at[part, target], grid.at[part, me], in_send.at[part], in_recv.at[part],
                device_id={"conf": target}, device_id_type=MESH,
            ).start()
            return carry

        lax.fori_loop(jnp.where(half == 0, 1, 0), 16, one, 0)

    reads[0].wait()
    pack(0, 0)
    pl.semaphore_wait(barrier, GROUP + 1)
    loads[0].wait()
    to_above = pltpu.make_async_remote_copy(
        velocity, halo.at[1], halo_send.at[0], halo_recv.at[1], device_id={"cell": above}, device_id_type=MESH
    )
    to_below = pltpu.make_async_remote_copy(
        velocity, halo.at[0], halo_send.at[1], halo_recv.at[0], device_id={"cell": below}, device_id_type=MESH
    )
    to_above.start()
    to_below.start()
    send_in(0, jnp.int32(0))
    for i in range(1, 4):
        reads[i].wait()
        pack(i // 2, i % 2)
        send_in(i // 2, jnp.int32(i % 2))
    for part in range(PARTS):
        pltpu.make_async_copy(packed.at[part, me], grid.at[part, me], in_recv.at[part]).start()

    to_above.wait()
    to_below.wait()
    last_row = velocity.shape[1] - 1
    gradients = [[], []]
    for i in range(2):
        here = velocity[i]
        along = (pltpu.roll(here, here.shape[1] - 1, 1) - pltpu.roll(here, 1, 1)) * 0.5
        down = (
            (here[1:2] - halo[0, i][last_row : last_row + 1]) * 0.5,
            (halo[1, i][0:1] - here[0:1]) * 0.5,
        )
        for part in range(PARTS):
            gradients[part] += [along[part : part + 1], down[part]]
    width = velocity.shape[2]
    filler = [jnp.zeros((4, width), jnp.float32)]
    gradients = [jnp.concatenate(one + filler, axis=0) for one in gradients]
    source = lax.broadcasted_iota(jnp.int32, (width, LANES), 0) - me * PART
    lane = lax.broadcasted_iota(jnp.int32, (width, LANES), 1)
    choose = (source == (lane & (PART - 1))).astype(jnp.float32)
    for part in range(PARTS):
        lanes[part] = exact_dot(gradients[part], choose)
    picked = jnp.where(me < GROUP // 2, gradients[0], gradients[1])
    offset = lax.rem(me, GROUP // 2) * OWN
    own_source = lax.broadcasted_iota(jnp.int32, (width, 128), 0) - offset
    own_lane = lax.broadcasted_iota(jnp.int32, (width, 128), 1)
    own = exact_dot(picked, ((own_source == own_lane) & (own_lane < OWN)).astype(jnp.float32))
    loads[1].wait()
    relaxed = relax(
        tuple(short[i : i + 1, :] for i in range(3)), tuple(own[i : i + 1, :OWN] for i in range(4))
    )
    for i in range(3):
        stress[i : i + 1, :OWN] = relaxed[i]
    build_operators(wa, wb, wc)

    coord_c = coord(lax.broadcasted_iota(jnp.int32, (1, 1, LANES), 2) // PART)
    coord_all = coord(lax.broadcasted_iota(jnp.int32, (1, Q, 1), 1))


    def build_springs(index, carry):
        here = coord(index)
        squares = here * here + coord_all * coord_all + coord_c * coord_c
        spring[pl.ds(index, 1)] = 1.0 / (1.0 - squares / fene_limit)
        return carry

    lax.fori_loop(0, Q, build_springs, 0)

    def advance(part, last):
        k11, k12, k21, k22 = (lanes[part, i : i + 1, :].reshape(1, 1, LANES) for i in range(4))

        def first_direction(tile, carry):
            window = pl.ds(pl.multiple_of(tile * 8, 8), 8)
            value = grid[part, :, window, :]
            coord_a = coord(lax.broadcasted_iota(jnp.int32, (Q, 1, 1), 0))
            coord_b = coord(lax.broadcasted_iota(jnp.int32, (1, 8, 1), 1) + tile * 8)
            drift = (k11 - diffusion * spring[:, window, :]) * coord_a + k12 * coord_b
            moved = (drift * value).reshape(Q * 8, LANES)
            terms = jnp.concatenate(split(moved) + split(value.reshape(Q * 8, LANES)), axis=0)
            result = jnp.dot(wa[...], terms, preferred_element_type=jnp.float32)
            change[:, window, :] = result.reshape(Q, 8, LANES)
            return carry

        lax.fori_loop(0, 4, first_direction, 0)

        def other_directions(tile, carry):
            window = pl.ds(tile * 8, 8)
            value = grid[part, window]
            stiff = spring[window]
            coord_a = coord(lax.broadcasted_iota(jnp.int32, (8, 1, 1), 0) + tile * 8)
            pull = diffusion * stiff
            drift_b = k21 * coord_a + (k22 - pull) * coord_all
            moved_b = (drift_b * value).reshape(8 * Q, LANES)
            moved_c = (-pull * coord_c * value).reshape(8 * Q, LANES)
            plain = split(value.reshape(8 * Q, LANES))
            terms_b = jnp.concatenate(split(moved_b) + plain, axis=0)
            part_b = jnp.dot(wb[...], terms_b, preferred_element_type=jnp.float32)
            terms_c = jnp.concatenate(split(moved_c) + plain, axis=1)
            part_c = jnp.dot(terms_c, wc[...], preferred_element_type=jnp.float32)
            value = value + (change[window] + (part_b + part_c).reshape(8, Q, LANES))
            grid[part, window] = value
            if last:
                weighted = stiff * value
                sums[0] += jnp.sum(weighted, axis=0)
                weighted = weighted * coord_a
                sums[1] += jnp.sum(weighted, axis=0)
                sums[2] += jnp.sum(weighted * coord_a, axis=0)
                sums[3] += jnp.sum(value, axis=0)
            return carry

        lax.fori_loop(0, 4, other_directions, 0)

    def whole(part, carry):
        pltpu.make_async_copy(grid.at[part], grid.at[part], in_recv.at[part]).wait()
        sums[...] = jnp.zeros_like(sums)
        for turn in range(STEPS):
            advance(part, turn == STEPS - 1)

        def send_to(arrived):
            def send_out(turn, inner):
                target = peer(turn // 16, lax.rem(turn, 16))
                pltpu.make_async_remote_copy(
                    grid.at[part, target], arrived.at[me], out_send.at[part], out_recv.at[part],
                    device_id={"conf": target}, device_id_type=MESH,
                ).start()
                return inner

            lax.fori_loop(1, GROUP, send_out, 0)
            pltpu.make_async_copy(grid.at[part, me], arrived.at[me], out_recv.at[part]).start()

        @pl.when(part == 0)
        def _():
            send_to(early_back)

        @pl.when(part == 1)
        def _():
            send_to(late)

        column = coord(lax.broadcasted_iota(jnp.int32, (Q, 1), 0))
        scale = 1.0 / float(Q**3)
        stacked = jnp.concatenate(
            [
                jnp.sum(sums[2], axis=0, keepdims=True),
                jnp.sum(sums[1] * column, axis=0, keepdims=True),
                jnp.sum(sums[0] * (column * column), axis=0, keepdims=True),
                jnp.sum(sums[3], axis=0, keepdims=True),
                jnp.zeros((4, LANES), jnp.float32),
            ],
            axis=0,
        )
        fold_row = lax.broadcasted_iota(jnp.int32, (LANES, 128), 0) & (PART - 1)
        fold_lane = lax.broadcasted_iota(jnp.int32, (LANES, 128), 1) - my_c * PART
        moments[part] = exact_dot(stacked * scale, (fold_row == fold_lane).astype(jnp.float32))
        owner = part * (GROUP // 2) + me // 2

        @pl.when(owner != me)
        def _():
            pltpu.make_async_remote_copy(
                moments.at[part], inbox.at[my_c], note_send.at[part], note_recv.at[my_c],
                device_id={"conf": owner}, device_id_type=MESH,
            ).start()

        @pl.when(owner == me)
        def _():
            pltpu.make_async_copy(moments.at[part], inbox.at[my_c], note_recv.at[my_c]).start()

        return carry

    lax.fori_loop(0, PARTS, whole, 0)

    for i in range(2):
        pltpu.make_async_copy(inbox.at[i], inbox.at[i], note_recv.at[i]).wait()
    total = inbox[0] + inbox[1]
    for i, polymer in enumerate(
        (
            polymer_eta * (total[0:1] - total[3:4]),
            polymer_eta * total[1:2],
            polymer_eta * (total[2:3] - total[3:4]),
        )
    ):
        stress[i + 4 : i + 5, :OWN] = polymer[:, :OWN] + stress[i : i + 1, :OWN]

    pltpu.make_async_copy(early_back, early_back, out_recv.at[0]).wait()

    def early_side(block, carry):
        unpack(early_back, early.at[block], block)
        early_write(block).start()
        return carry

    def early_write(block):
        return pltpu.make_async_copy(early.at[block], early_hbm.at[block], write_sem.at[block])

    lax.fori_loop(0, 2, early_side, 0)
    pltpu.make_async_copy(late, late, out_recv.at[1]).wait()
    for i in range(2):
        early_write(i).wait()
    others = pl.ds(0, GROUP - 1)
    for part in range(PARTS):
        pltpu.make_async_copy(packed.at[part, others], packed.at[part, others], in_send.at[part]).wait()
        pltpu.make_async_copy(grid.at[part, others], grid.at[part, others], out_send.at[part]).wait()

        @pl.when(part * (GROUP // 2) + me // 2 != me)
        def _(part=part):
            pltpu.make_async_copy(moments.at[part], moments.at[part], note_send.at[part]).wait()


def spread(early_hbm, late_hbm, stress, out_hbm, short_hbm, total_hbm, early, late, out, small, sem):
    loads = [
        pltpu.make_async_copy(late_hbm.at[pl.ds(16 * i, 16)], late.at[pl.ds(16 * i, 16)], sem.at[i]) for i in range(2)
    ]
    loads += [pltpu.make_async_copy(early_hbm.at[i], early.at[i], sem.at[2 + i]) for i in range(2)]
    for load in loads:
        load.start()
    for i in range(2):
        small[i] = stress[4 * i : 4 * i + 3, :OWN]
    copies = [
        pltpu.make_async_copy(small.at[i], target, sem.at[4 + i]) for i, target in enumerate((short_hbm, total_hbm))
    ]
    for copy in copies:
        copy.start()
    for i in range(2):
        loads[i].wait()
        unpack(late, out.at[i], i)
        loads[2 + i].wait()
        for j, source in enumerate((out, early)):
            columns = pl.ds((256 if j == 0 else 0) + i * 128, 128)
            copy = pltpu.make_async_copy(source.at[i], out_hbm.at[:, columns], sem.at[6 + 2 * i + j])
            copy.start()
            copies.append(copy)
    for copy in copies:
        copy.wait()


def on_device(density, velocity, short_stress):
    vmem = pl.BlockSpec(memory_space=pltpu.VMEM)
    hbm = pl.BlockSpec(memory_space=pltpu.HBM)
    blocks = (PARTS, GROUP, Q, LANES)
    dma = pltpu.SemaphoreType.DMA
    early, late, stress = pl.pallas_call(
        kernel,
        name="fokker_planck",
        out_shape=(
            jax.ShapeDtypeStruct((2, Q * Q, 128), jnp.float32),
            jax.ShapeDtypeStruct((GROUP, Q, LANES), jnp.float32),
            jax.ShapeDtypeStruct((8, 128), jnp.float32),
        ),
        in_specs=[hbm] * 3,
        out_specs=(hbm, vmem, vmem),
        scratch_shapes=[
            pltpu.VMEM((4, Q * Q, 128), jnp.float32),
            pltpu.VMEM(velocity.shape, jnp.float32),
            pltpu.VMEM(short_stress.shape, jnp.float32),
            pltpu.VMEM((2, Q * Q, 128), jnp.float32),
            pltpu.VMEM((GROUP, Q, LANES), jnp.float32),
            pltpu.VMEM((2, 8, 128), jnp.float32),
            pltpu.VMEM(blocks, jnp.float32),
            pltpu.VMEM(blocks, jnp.float32),
            pltpu.VMEM((Q, Q, LANES), jnp.float32),
            pltpu.VMEM((Q, Q, LANES), jnp.float32),
            pltpu.VMEM((8 * Q, 6 * 8 * Q), jnp.bfloat16),
            pltpu.VMEM((8 * Q, 6 * 8 * Q), jnp.bfloat16),
            pltpu.VMEM((6 * LANES, LANES), jnp.bfloat16),
            pltpu.VMEM((2,) + velocity.shape, jnp.float32),
            pltpu.VMEM((PARTS, 8, LANES), jnp.float32),
            pltpu.VMEM((4, Q, LANES), jnp.float32),
            pltpu.VMEM((PARTS, 8, 128), jnp.float32),
            dma((PARTS,)),
            dma((PARTS,)),
            dma((PARTS,)),
            dma((PARTS,)),
            dma((2,)),
            dma((2,)),
            dma((2,)),
            dma((4,)),
            dma((PARTS,)),
            dma((2,)),
            dma((2,)),
        ],
        compiler_params=pltpu.CompilerParams(
            collective_id=0, has_side_effects=True, vmem_limit_bytes=VMEM_LIMIT
        ),
    )(
        density.reshape(Q * Q, CELLS),
        velocity,
        short_stress,
    )
    result, short_next, total_stress = pl.pallas_call(
        spread,
        name="spread",
        out_shape=(
            jax.ShapeDtypeStruct((Q * Q, CELLS), jnp.float32),
            jax.ShapeDtypeStruct(short_stress.shape, jnp.float32),
            jax.ShapeDtypeStruct(short_stress.shape, jnp.float32),
        ),
        in_specs=[hbm, hbm, vmem],
        out_specs=(hbm, hbm, hbm),
        scratch_shapes=[
            pltpu.VMEM((2, Q * Q, 128), jnp.float32),
            pltpu.VMEM((GROUP, Q, LANES), jnp.float32),
            pltpu.VMEM((2, Q * Q, 128), jnp.float32),
            pltpu.VMEM((2,) + short_stress.shape, jnp.float32),
            dma((10,)),
        ],
        compiler_params=pltpu.CompilerParams(vmem_limit_bytes=VMEM_LIMIT),
    )(early, late, stress)
    return result.reshape(density.shape), short_next, total_stress


def solution(mesh):
    return jax.shard_map(
        on_device,
        mesh=mesh,
        in_specs=(P("conf", None, None, "cell"), P(None, "cell", None), P(None, ("cell", "conf"))),
        out_specs=(
            P("conf", None, None, "cell"),
            P(None, ("cell", "conf")),
            P(None, ("cell", "conf")),
        ),
        check_vma=False,
    )
```

```python
import functools

import jax
import jax.numpy as jnp
import numpy as np
from jax import lax
from jax.experimental import pallas as pl
from jax.experimental.pallas import tpu as pltpu
from jax.sharding import PartitionSpec as P

STEPS = 2
half_extent = 3.0
fene_limit = 50.0
diffusion = 0.5
time_step = 0.001
polymer_eta = 1.0
solvent_eta = 0.5
short_relax = 0.01

MESH = pl.DeviceIdType.MESH
Q = 32
GROUP = 32
OWN = 16
PART = 8
PARTS = 2
LANES = Q * PART
CELLS = GROUP * OWN
TALL = 32
VMEM_LIMIT = 50 * 1024 * 1024


def stencils():
    offsets = np.arange(Q)[:, None] - np.arange(Q)[None, :]
    angle = offsets * (np.pi / Q)
    sine = np.where(offsets == 0, 1.0, np.sin(angle))
    first = np.where(offsets % 2 == 0, 1.0, -1.0) * np.cos(angle) / sine * (np.pi / (2 * half_extent))
    first = np.where(offsets == 0, 0.0, first)
    return (-time_step * first)[:, 0], (time_step * diffusion * (first @ first))[:, 0]


def build_operators(wa, wb, wc):
    first, second = stencils()
    size = 8 * Q
    row = lax.broadcasted_iota(jnp.int32, (size, size), 0)
    column = lax.broadcasted_iota(jnp.int32, (size, size), 1)

    def circulant(offset, inside):
        key = jnp.where(inside, offset & (Q - 1), -1)
        one, two = (jnp.zeros((size, size), jnp.float32) for _ in range(2))
        for i in range(Q):
            here = key == i
            one = jnp.where(here, jnp.float32(first[i]), one)
            two = jnp.where(here, jnp.float32(second[i]), two)
        return one, two

    def store(ref, matrix, at, by_row):
        high, low, again = split(matrix)
        for i, value in enumerate((high, again, low)):
            place = pl.ds((at + i) * size, size)
            if by_row:
                ref[place, :] = value
            else:
                ref[:, place] = value

    one, two = circulant((row >> 3) - (column >> 3), (row & 7) == (column & 7))
    store(wa, one, 0, False)
    store(wa, two, 3, False)
    store(wc, -one, 0, True)
    store(wc, two, 3, True)
    one, two = circulant(row - column, (row >> 5) == (column >> 5))
    store(wb, one, 0, False)
    store(wb, two, 3, False)


def coord(index):
    return -half_extent + (index.astype(jnp.float32) + 0.5) * (2.0 * half_extent / Q)


def split(value):
    high = value.astype(jnp.bfloat16)
    low = (value - high.astype(jnp.float32)).astype(jnp.bfloat16)
    return [high, low, high]


def exchange_lanes(values):
    lane = lax.broadcasted_iota(jnp.int32, values[0].shape, 1)
    values = list(values)
    for bit in (1, 2, 4, 8):
        upper = (lane & (8 * bit)) != 0
        shift = 8 * bit
        for i in range(16):
            if i & bit:
                continue
            one, two = values[i], values[i | bit]
            mixed = jnp.where(upper, one, two)
            if shift == 64:
                mixed = pltpu.roll(mixed, 64, 1)
            else:
                mixed = jnp.take_along_axis(mixed, lane ^ shift, axis=1, mode="promise_in_bounds")
            values[i] = jnp.where(upper, mixed, one)
            values[i | bit] = jnp.where(upper, two, mixed)
    return values


def unpack(arrived, target, block):
    def piece(turn, carry):
        tile, half = turn // 2, turn % 2
        values = [
            arrived[
                block * 16 + i, pl.ds(pl.multiple_of(tile * TALL, TALL), TALL),
                pl.ds(pl.multiple_of(half * 128, 128), 128),
            ]
            for i in range(16)
        ]
        values = exchange_lanes(values)
        for i in range(16):
            target[pl.ds(tile * (TALL * Q) + half * 16 + i, TALL, stride=Q), :] = values[i]
        return carry

    lax.fori_loop(0, 2 * Q // TALL, piece, 0)


def exact_dot(one, two):
    return jnp.dot(one, two, precision=lax.Precision.HIGHEST, preferred_element_type=jnp.float32)


def relax(stress, gradient):
    stress_xx, stress_xy, stress_yy = stress
    for _ in range(STEPS):
        next_xx = stress_xx + time_step * (
            2.0 * (gradient[0] * stress_xx + gradient[1] * stress_xy)
            - (stress_xx - 2.0 * solvent_eta * gradient[0]) / short_relax
        )
        next_xy = stress_xy + time_step * (
            gradient[0] * stress_xy
            + gradient[1] * stress_yy
            + gradient[2] * stress_xx
            + gradient[3] * stress_xy
            - (stress_xy - solvent_eta * (gradient[1] + gradient[2])) / short_relax
        )
        next_yy = stress_yy + time_step * (
            2.0 * (gradient[2] * stress_xy + gradient[3] * stress_yy)
            - (stress_yy - 2.0 * solvent_eta * gradient[3]) / short_relax
        )
        stress_xx, stress_xy, stress_yy = next_xx, next_xy, next_yy
    return stress_xx, stress_xy, stress_yy


def kernel(
    density_hbm, velocity_hbm, short_hbm,
    early, late, stress,
    density, velocity, short, early_back, inbox, packed, grid, change, spring, wa, wb, wc, halo, lanes, sums, moments,
    in_send, in_recv, out_send, out_recv, load_sem, halo_send, halo_recv, read_sem,
    note_send, note_recv,
):
    me = lax.axis_index("conf")
    my_y, my_z, my_c = me // 8, (me // 2) % 4, me % 2
    brick = lax.axis_index("cell")
    bricks = lax.axis_size("cell")
    above, below = lax.rem(brick + bricks - 1, bricks), lax.rem(brick + 1, bricks)

    reads = [
        pltpu.make_async_copy(
            density_hbm.at[:, pl.ds(pl.multiple_of(block * 128, 128), 128)], density.at[block], read_sem.at[i]
        )
        for i, block in enumerate([2 * (i // 2) + lax.rem(my_y // 2 + i, 2) for i in range(4)])
    ]
    for read in reads:
        read.start()
    barrier = pltpu.get_barrier_semaphore()

    def greet(turn, carry):
        pl.semaphore_signal(barrier, inc=1, device_id={"conf": lax.rem(me + turn, GROUP)}, device_id_type=MESH)
        return carry

    lax.fori_loop(1, GROUP, greet, 0)
    for other in (above, below):
        pl.semaphore_signal(barrier, inc=1, device_id={"cell": other}, device_id_type=MESH)

    loads = [
        pltpu.make_async_copy(source, target, load_sem.at[i])
        for i, (source, target) in enumerate(
            ((velocity_hbm, velocity), (short_hbm, short))
        )
    ]
    for load in loads:
        load.start()

    def side(turn):
        return lax.rem(my_y // 2 + turn, 2)

    def peer(half, turn):
        y = 2 * side(half) + lax.rem(my_y + turn // 8, 2)
        z = lax.rem(my_z + lax.rem(turn, 8) // 2, 4)
        return y * 8 + z * 2 + lax.rem(my_c + turn, 2)

    def pack(part, half):
        first = side(half)
        block = part * 2 + first

        def piece(turn, carry):
            tile, half = turn // 2, turn % 2
            values = [
                density[block, pl.ds(tile * (TALL * Q) + half * 16 + i, TALL, stride=Q), :] for i in range(16)
            ]
            values = exchange_lanes(values)
            for i in range(16):
                packed[
                    part, first * 16 + i, pl.ds(pl.multiple_of(tile * TALL, TALL), TALL),
                    pl.ds(pl.multiple_of(half * 128, 128), 128),
                ] = values[i]
            return carry

        lax.fori_loop(0, 2 * Q // TALL, piece, 0)

    def send_in(part, half):
        def one(turn, carry):
            target = peer(half, turn)
            pltpu.make_async_remote_copy(
                packed.at[part, target], grid.at[part, me], in_send.at[part], in_recv.at[part],
                device_id={"conf": target}, device_id_type=MESH,
            ).start()
            return carry

        lax.fori_loop(jnp.where(half == 0, 1, 0), 16, one, 0)

    reads[0].wait()
    pack(0, 0)
    pl.semaphore_wait(barrier, GROUP + 1)
    loads[0].wait()
    to_above = pltpu.make_async_remote_copy(
        velocity, halo.at[1], halo_send.at[0], halo_recv.at[1], device_id={"cell": above}, device_id_type=MESH
    )
    to_below = pltpu.make_async_remote_copy(
        velocity, halo.at[0], halo_send.at[1], halo_recv.at[0], device_id={"cell": below}, device_id_type=MESH
    )
    to_above.start()
    to_below.start()
    send_in(0, jnp.int32(0))
    for i in range(1, 4):
        reads[i].wait()
        pack(i // 2, i % 2)
        send_in(i // 2, jnp.int32(i % 2))
    for part in range(PARTS):
        pltpu.make_async_copy(packed.at[part, me], grid.at[part, me], in_recv.at[part]).start()

    to_above.wait()
    to_below.wait()
    last_row = velocity.shape[1] - 1
    gradients = [[], []]
    for i in range(2):
        here = velocity[i]
        along = (pltpu.roll(here, here.shape[1] - 1, 1) - pltpu.roll(here, 1, 1)) * 0.5
        down = (
            (here[1:2] - halo[0, i][last_row : last_row + 1]) * 0.5,
            (halo[1, i][0:1] - here[0:1]) * 0.5,
        )
        for part in range(PARTS):
            gradients[part] += [along[part : part + 1], down[part]]
    width = velocity.shape[2]
    filler = [jnp.zeros((4, width), jnp.float32)]
    gradients = [jnp.concatenate(one + filler, axis=0) for one in gradients]
    source = lax.broadcasted_iota(jnp.int32, (width, LANES), 0) - me * PART
    lane = lax.broadcasted_iota(jnp.int32, (width, LANES), 1)
    choose = (source == (lane & (PART - 1))).astype(jnp.float32)
    for part in range(PARTS):
        lanes[part] = exact_dot(gradients[part], choose)
    picked = jnp.where(me < GROUP // 2, gradients[0], gradients[1])
    offset = lax.rem(me, GROUP // 2) * OWN
    own_source = lax.broadcasted_iota(jnp.int32, (width, 128), 0) - offset
    own_lane = lax.broadcasted_iota(jnp.int32, (width, 128), 1)
    own = exact_dot(picked, ((own_source == own_lane) & (own_lane < OWN)).astype(jnp.float32))
    loads[1].wait()
    relaxed = relax(
        tuple(short[i : i + 1, :] for i in range(3)), tuple(own[i : i + 1, :OWN] for i in range(4))
    )
    for i in range(3):
        stress[i : i + 1, :OWN] = relaxed[i]
    build_operators(wa, wb, wc)

    coord_c = coord(lax.broadcasted_iota(jnp.int32, (1, 1, LANES), 2) // PART)
    coord_all = coord(lax.broadcasted_iota(jnp.int32, (1, Q, 1), 1))


    def build_springs(index, carry):
        here = coord(index)
        squares = here * here + coord_all * coord_all + coord_c * coord_c
        spring[pl.ds(index, 1)] = 1.0 / (1.0 - squares / fene_limit)
        return carry

    lax.fori_loop(0, Q, build_springs, 0)

    def advance(part, last):
        k11, k12, k21, k22 = (lanes[part, i : i + 1, :].reshape(1, 1, LANES) for i in range(4))

        def first_direction(tile, carry):
            window = pl.ds(pl.multiple_of(tile * 8, 8), 8)
            value = grid[part, :, window, :]
            coord_a = coord(lax.broadcasted_iota(jnp.int32, (Q, 1, 1), 0))
            coord_b = coord(lax.broadcasted_iota(jnp.int32, (1, 8, 1), 1) + tile * 8)
            drift = (k11 - diffusion * spring[:, window, :]) * coord_a + k12 * coord_b
            moved = (drift * value).reshape(Q * 8, LANES)
            terms = jnp.concatenate(split(moved) + split(value.reshape(Q * 8, LANES)), axis=0)
            result = jnp.dot(wa[...], terms, preferred_element_type=jnp.float32)
            change[:, window, :] = result.reshape(Q, 8, LANES)
            return carry

        lax.fori_loop(0, 4, first_direction, 0)

        def other_directions(tile, carry):
            window = pl.ds(tile * 8, 8)
            value = grid[part, window]
            stiff = spring[window]
            coord_a = coord(lax.broadcasted_iota(jnp.int32, (8, 1, 1), 0) + tile * 8)
            pull = diffusion * stiff
            drift_b = k21 * coord_a + (k22 - pull) * coord_all
            moved_b = (drift_b * value).reshape(8 * Q, LANES)
            moved_c = (-pull * coord_c * value).reshape(8 * Q, LANES)
            plain = split(value.reshape(8 * Q, LANES))
            terms_b = jnp.concatenate(split(moved_b) + plain, axis=0)
            part_b = jnp.dot(wb[...], terms_b, preferred_element_type=jnp.float32)
            terms_c = jnp.concatenate(split(moved_c) + plain, axis=1)
            part_c = jnp.dot(terms_c, wc[...], preferred_element_type=jnp.float32)
            value = value + (change[window] + (part_b + part_c).reshape(8, Q, LANES))
            grid[part, window] = value
            if last:
                weighted = stiff * value
                sums[0] += jnp.sum(weighted, axis=0)
                weighted = weighted * coord_a
                sums[1] += jnp.sum(weighted, axis=0)
                sums[2] += jnp.sum(weighted * coord_a, axis=0)
                sums[3] += jnp.sum(value, axis=0)
            return carry

        lax.fori_loop(0, 4, other_directions, 0)

    def whole(part, carry):
        pltpu.make_async_copy(grid.at[part], grid.at[part], in_recv.at[part]).wait()
        sums[...] = jnp.zeros_like(sums)
        for turn in range(STEPS):
            advance(part, turn == STEPS - 1)

        def send_to(arrived):
            def send_out(turn, inner):
                target = peer(turn // 16, lax.rem(turn, 16))
                pltpu.make_async_remote_copy(
                    grid.at[part, target], arrived.at[me], out_send.at[part], out_recv.at[part],
                    device_id={"conf": target}, device_id_type=MESH,
                ).start()
                return inner

            lax.fori_loop(1, GROUP, send_out, 0)
            pltpu.make_async_copy(grid.at[part, me], arrived.at[me], out_recv.at[part]).start()

        @pl.when(part == 0)
        def _():
            send_to(early_back)

        @pl.when(part == 1)
        def _():
            send_to(late)

        column = coord(lax.broadcasted_iota(jnp.int32, (Q, 1), 0))
        scale = 1.0 / float(Q**3)
        stacked = jnp.concatenate(
            [
                jnp.sum(sums[2], axis=0, keepdims=True),
                jnp.sum(sums[1] * column, axis=0, keepdims=True),
                jnp.sum(sums[0] * (column * column), axis=0, keepdims=True),
                jnp.sum(sums[3], axis=0, keepdims=True),
                jnp.zeros((4, LANES), jnp.float32),
            ],
            axis=0,
        )
        fold_row = lax.broadcasted_iota(jnp.int32, (LANES, 128), 0) & (PART - 1)
        fold_lane = lax.broadcasted_iota(jnp.int32, (LANES, 128), 1) - my_c * PART
        moments[part] = exact_dot(stacked * scale, (fold_row == fold_lane).astype(jnp.float32))
        owner = part * (GROUP // 2) + me // 2

        @pl.when(owner != me)
        def _():
            pltpu.make_async_remote_copy(
                moments.at[part], inbox.at[my_c], note_send.at[part], note_recv.at[my_c],
                device_id={"conf": owner}, device_id_type=MESH,
            ).start()

        @pl.when(owner == me)
        def _():
            pltpu.make_async_copy(moments.at[part], inbox.at[my_c], note_recv.at[my_c]).start()

        return carry

    lax.fori_loop(0, PARTS, whole, 0)

    for i in range(2):
        pltpu.make_async_copy(inbox.at[i], inbox.at[i], note_recv.at[i]).wait()
    total = inbox[0] + inbox[1]
    for i, polymer in enumerate(
        (
            polymer_eta * (total[0:1] - total[3:4]),
            polymer_eta * total[1:2],
            polymer_eta * (total[2:3] - total[3:4]),
        )
    ):
        stress[i + 4 : i + 5, :OWN] = polymer[:, :OWN] + stress[i : i + 1, :OWN]

    pltpu.make_async_copy(early_back, early_back, out_recv.at[0]).wait()

    def early_side(block, carry):
        unpack(early_back, early.at[block], block)
        return carry

    lax.fori_loop(0, 2, early_side, 0)
    pltpu.make_async_copy(late, late, out_recv.at[1]).wait()
    others = pl.ds(0, GROUP - 1)
    for part in range(PARTS):
        pltpu.make_async_copy(packed.at[part, others], packed.at[part, others], in_send.at[part]).wait()
        pltpu.make_async_copy(grid.at[part, others], grid.at[part, others], out_send.at[part]).wait()

        @pl.when(part * (GROUP // 2) + me // 2 != me)
        def _(part=part):
            pltpu.make_async_copy(moments.at[part], moments.at[part], note_send.at[part]).wait()


def spread(early, late, stress, out_hbm, short_hbm, total_hbm, out, small, sem):
    copies = [
        pltpu.make_async_copy(early.at[i], out_hbm.at[:, pl.ds(i * 128, 128)], sem.at[i]) for i in range(2)
    ]
    for copy in copies:
        copy.start()
    for i, target in enumerate((short_hbm, total_hbm)):
        small[i] = stress[4 * i : 4 * i + 3, :OWN]
        copies.append(pltpu.make_async_copy(small.at[i], target, sem.at[2 + i]))
        copies[-1].start()
    for i in range(2):
        unpack(late, out.at[i], i)
        copies.append(
            pltpu.make_async_copy(out.at[i], out_hbm.at[:, pl.ds(256 + i * 128, 128)], sem.at[4 + i])
        )
        copies[-1].start()
    for copy in copies:
        copy.wait()


def on_device(density, velocity, short_stress):
    vmem = pl.BlockSpec(memory_space=pltpu.VMEM)
    hbm = pl.BlockSpec(memory_space=pltpu.HBM)
    blocks = (PARTS, GROUP, Q, LANES)
    dma = pltpu.SemaphoreType.DMA
    early, late, stress = pl.pallas_call(
        kernel,
        name="fokker_planck",
        out_shape=(
            jax.ShapeDtypeStruct((2, Q * Q, 128), jnp.float32),
            jax.ShapeDtypeStruct((GROUP, Q, LANES), jnp.float32),
            jax.ShapeDtypeStruct((8, 128), jnp.float32),
        ),
        in_specs=[hbm] * 3,
        out_specs=(vmem, vmem, vmem),
        scratch_shapes=[
            pltpu.VMEM((4, Q * Q, 128), jnp.float32),
            pltpu.VMEM(velocity.shape, jnp.float32),
            pltpu.VMEM(short_stress.shape, jnp.float32),
            pltpu.VMEM((GROUP, Q, LANES), jnp.float32),
            pltpu.VMEM((2, 8, 128), jnp.float32),
            pltpu.VMEM(blocks, jnp.float32),
            pltpu.VMEM(blocks, jnp.float32),
            pltpu.VMEM((Q, Q, LANES), jnp.float32),
            pltpu.VMEM((Q, Q, LANES), jnp.float32),
            pltpu.VMEM((8 * Q, 6 * 8 * Q), jnp.bfloat16),
            pltpu.VMEM((8 * Q, 6 * 8 * Q), jnp.bfloat16),
            pltpu.VMEM((6 * LANES, LANES), jnp.bfloat16),
            pltpu.VMEM((2,) + velocity.shape, jnp.float32),
            pltpu.VMEM((PARTS, 8, LANES), jnp.float32),
            pltpu.VMEM((4, Q, LANES), jnp.float32),
            pltpu.VMEM((PARTS, 8, 128), jnp.float32),
            dma((PARTS,)),
            dma((PARTS,)),
            dma((PARTS,)),
            dma((PARTS,)),
            dma((2,)),
            dma((2,)),
            dma((2,)),
            dma((4,)),
            dma((PARTS,)),
            dma((2,)),
        ],
        compiler_params=pltpu.CompilerParams(
            collective_id=0, has_side_effects=True, vmem_limit_bytes=VMEM_LIMIT
        ),
    )(
        *(
            pltpu.with_memory_space_constraint(one, pltpu.HBM)
            for one in (density.reshape(Q * Q, CELLS), velocity, short_stress)
        ),
    )
    result, short_next, total_stress = pl.pallas_call(
        spread,
        name="spread",
        out_shape=(
            jax.ShapeDtypeStruct((Q * Q, CELLS), jnp.float32),
            jax.ShapeDtypeStruct(short_stress.shape, jnp.float32),
            jax.ShapeDtypeStruct(short_stress.shape, jnp.float32),
        ),
        in_specs=[vmem, vmem, vmem],
        out_specs=(hbm, hbm, hbm),
        scratch_shapes=[
            pltpu.VMEM((2, Q * Q, 128), jnp.float32),
            pltpu.VMEM((2,) + short_stress.shape, jnp.float32),
            dma((6,)),
        ],
        compiler_params=pltpu.CompilerParams(vmem_limit_bytes=VMEM_LIMIT),
    )(early, late, stress)
    return result.reshape(density.shape), short_next, total_stress


def solution(mesh):
    return jax.shard_map(
        on_device,
        mesh=mesh,
        in_specs=(P("conf", None, None, "cell"), P(None, "cell", None), P(None, ("cell", "conf"))),
        out_specs=(
            P("conf", None, None, "cell"),
            P(None, ("cell", "conf")),
            P(None, ("cell", "conf")),
        ),
        check_vma=False,
    )
```

```python
import functools

import jax
import jax.numpy as jnp
import numpy as np
from jax import lax
from jax.experimental import pallas as pl
from jax.experimental.pallas import tpu as pltpu
from jax.sharding import PartitionSpec as P

STEPS = 2
half_extent = 3.0
fene_limit = 50.0
diffusion = 0.5
time_step = 0.001
polymer_eta = 1.0
solvent_eta = 0.5
short_relax = 0.01

MESH = pl.DeviceIdType.MESH
Q = 32
GROUP = 32
OWN = 16
PART = 8
PARTS = 2
LANES = Q * PART
CELLS = GROUP * OWN
TALL = 32
VMEM_LIMIT = 50 * 1024 * 1024


def stencils():
    offsets = np.arange(Q)[:, None] - np.arange(Q)[None, :]
    angle = offsets * (np.pi / Q)
    sine = np.where(offsets == 0, 1.0, np.sin(angle))
    first = np.where(offsets % 2 == 0, 1.0, -1.0) * np.cos(angle) / sine * (np.pi / (2 * half_extent))
    first = np.where(offsets == 0, 0.0, first)
    return (-time_step * first)[:, 0], (time_step * diffusion * (first @ first))[:, 0]


def build_operators(wa, wb, wc):
    first, second = stencils()
    size = 8 * Q
    row = lax.broadcasted_iota(jnp.int32, (size, size), 0)
    column = lax.broadcasted_iota(jnp.int32, (size, size), 1)

    def circulant(offset, inside):
        key = jnp.where(inside, offset & (Q - 1), -1)
        one, two = (jnp.zeros((size, size), jnp.float32) for _ in range(2))
        for i in range(Q):
            here = key == i
            one = jnp.where(here, jnp.float32(first[i]), one)
            two = jnp.where(here, jnp.float32(second[i]), two)
        return one, two

    def store(ref, matrix, at, by_row):
        high, low, again = split(matrix)
        for i, value in enumerate((high, again, low)):
            place = pl.ds((at + i) * size, size)
            if by_row:
                ref[place, :] = value
            else:
                ref[:, place] = value

    one, two = circulant((row >> 3) - (column >> 3), (row & 7) == (column & 7))
    store(wa, one, 0, False)
    store(wa, two, 3, False)
    store(wc, -one, 0, True)
    store(wc, two, 3, True)
    one, two = circulant(row - column, (row >> 5) == (column >> 5))
    store(wb, one, 0, False)
    store(wb, two, 3, False)


def coord(index):
    return -half_extent + (index.astype(jnp.float32) + 0.5) * (2.0 * half_extent / Q)


def split(value):
    high = value.astype(jnp.bfloat16)
    low = (value - high.astype(jnp.float32)).astype(jnp.bfloat16)
    return [high, low, high]


def exchange_lanes(values):
    lane = lax.broadcasted_iota(jnp.int32, values[0].shape, 1)
    values = list(values)
    for bit in (1, 2, 4, 8):
        upper = (lane & (8 * bit)) != 0
        shift = 8 * bit
        for i in range(16):
            if i & bit:
                continue
            one, two = values[i], values[i | bit]
            mixed = jnp.where(upper, one, two)
            if shift == 64:
                mixed = pltpu.roll(mixed, 64, 1)
            else:
                mixed = jnp.take_along_axis(mixed, lane ^ shift, axis=1, mode="promise_in_bounds")
            values[i] = jnp.where(upper, mixed, one)
            values[i | bit] = jnp.where(upper, two, mixed)
    return values


def unpack(arrived, target, block):
    def piece(turn, carry):
        tile, half = turn // 2, turn % 2
        values = [
            arrived[
                block * 16 + i, pl.ds(tile * TALL, TALL),
                pl.ds(half * 128, 128),
            ]
            for i in range(16)
        ]
        values = exchange_lanes(values)
        for i in range(16):
            target[pl.ds(tile * (TALL * Q) + half * 16 + i, TALL, stride=Q), :] = values[i]
        return carry

    for turn in range(2 * Q // TALL):
        piece(turn, 0)


def exact_dot(one, two):
    return jnp.dot(one, two, precision=lax.Precision.HIGHEST, preferred_element_type=jnp.float32)


def relax(stress, gradient):
    stress_xx, stress_xy, stress_yy = stress
    for _ in range(STEPS):
        next_xx = stress_xx + time_step * (
            2.0 * (gradient[0] * stress_xx + gradient[1] * stress_xy)
            - (stress_xx - 2.0 * solvent_eta * gradient[0]) / short_relax
        )
        next_xy = stress_xy + time_step * (
            gradient[0] * stress_xy
            + gradient[1] * stress_yy
            + gradient[2] * stress_xx
            + gradient[3] * stress_xy
            - (stress_xy - solvent_eta * (gradient[1] + gradient[2])) / short_relax
        )
        next_yy = stress_yy + time_step * (
            2.0 * (gradient[2] * stress_xy + gradient[3] * stress_yy)
            - (stress_yy - 2.0 * solvent_eta * gradient[3]) / short_relax
        )
        stress_xx, stress_xy, stress_yy = next_xx, next_xy, next_yy
    return stress_xx, stress_xy, stress_yy


def kernel(
    density_hbm, velocity_hbm, short_hbm,
    early, late, stress,
    density, velocity, short, early_back, near_back, inbox, packed, grid, change, spring, wa, wb, wc, halo, lanes, sums, moments,
    in_send, in_recv, out_send, out_recv, load_sem, halo_send, halo_recv, read_sem,
    note_send, note_recv,
):
    me = lax.axis_index("conf")
    my_y, my_z, my_c = me // 8, (me // 2) % 4, me % 2
    brick = lax.axis_index("cell")
    bricks = lax.axis_size("cell")
    above, below = lax.rem(brick + bricks - 1, bricks), lax.rem(brick + 1, bricks)

    reads = [
        pltpu.make_async_copy(
            density_hbm.at[:, pl.ds(pl.multiple_of(block * 128, 128), 128)], density.at[block], read_sem.at[i]
        )
        for i, block in enumerate([2 * (i // 2) + lax.rem(my_y // 2 + i, 2) for i in range(4)])
    ]
    reads[0].start()
    barrier = pltpu.get_barrier_semaphore()

    for turn in range(1, GROUP):
        pl.semaphore_signal(barrier, inc=1, device_id={"conf": lax.rem(me + turn, GROUP)}, device_id_type=MESH)
    for other in (above, below):
        pl.semaphore_signal(barrier, inc=1, device_id={"cell": other}, device_id_type=MESH)

    for read in reads[1:]:
        read.start()
    loads = [
        pltpu.make_async_copy(source, target, load_sem.at[i])
        for i, (source, target) in enumerate(
            ((velocity_hbm, velocity), (short_hbm, short))
        )
    ]
    for load in loads:
        load.start()

    def side(turn):
        return lax.rem(my_y // 2 + turn, 2)

    def peer(half, turn):
        y = 2 * side(half) + lax.rem(my_y + turn // 8, 2)
        z = lax.rem(my_z + lax.rem(turn, 8) // 2, 4)
        return y * 8 + z * 2 + lax.rem(my_c + turn, 2)

    def pack(part, half):
        first = side(half)
        block = part * 2 + first

        def piece(turn, carry):
            tile, half = turn // 2, turn % 2
            values = [
                density[block, pl.ds(tile * (TALL * Q) + half * 16 + i, TALL, stride=Q), :] for i in range(16)
            ]
            values = exchange_lanes(values)
            for i in range(16):
                packed[
                    part, first * 16 + i, pl.ds(tile * TALL, TALL),
                    pl.ds(half * 128, 128),
                ] = values[i]
            return carry

        for turn in range(2 * Q // TALL):
            piece(turn, 0)

    def send_in(part, half):
        def one(turn, carry):
            target = peer(half, turn)
            pltpu.make_async_remote_copy(
                packed.at[part, target], grid.at[part, me], in_send.at[part], in_recv.at[part],
                device_id={"conf": target}, device_id_type=MESH,
            ).start()
            return carry

        lax.fori_loop(jnp.where(half == 0, 1, 0), 16, one, 0)

    reads[0].wait()
    pack(0, 0)
    pl.semaphore_wait(barrier, GROUP + 1)
    loads[0].wait()
    to_above = pltpu.make_async_remote_copy(
        velocity, halo.at[1], halo_send.at[0], halo_recv.at[1], device_id={"cell": above}, device_id_type=MESH
    )
    to_below = pltpu.make_async_remote_copy(
        velocity, halo.at[0], halo_send.at[1], halo_recv.at[0], device_id={"cell": below}, device_id_type=MESH
    )
    to_above.start()
    to_below.start()
    send_in(0, jnp.int32(0))
    for i in range(1, 4):
        reads[i].wait()
        pack(i // 2, i % 2)
        send_in(i // 2, jnp.int32(i % 2))
    for part in range(PARTS):
        pltpu.make_async_copy(packed.at[part, me], grid.at[part, me], in_recv.at[part]).start()

    to_above.wait()
    to_below.wait()
    last_row = velocity.shape[1] - 1
    gradients = [[], []]
    for i in range(2):
        here = velocity[i]
        along = (pltpu.roll(here, here.shape[1] - 1, 1) - pltpu.roll(here, 1, 1)) * 0.5
        down = (
            (here[1:2] - halo[0, i][last_row : last_row + 1]) * 0.5,
            (halo[1, i][0:1] - here[0:1]) * 0.5,
        )
        for part in range(PARTS):
            gradients[part] += [along[part : part + 1], down[part]]
    width = velocity.shape[2]
    filler = [jnp.zeros((4, width), jnp.float32)]
    gradients = [jnp.concatenate(one + filler, axis=0) for one in gradients]
    source = lax.broadcasted_iota(jnp.int32, (width, LANES), 0) - me * PART
    lane = lax.broadcasted_iota(jnp.int32, (width, LANES), 1)
    choose = (source == (lane & (PART - 1))).astype(jnp.float32)
    for part in range(PARTS):
        lanes[part] = exact_dot(gradients[part], choose)
    picked = jnp.where(me < GROUP // 2, gradients[0], gradients[1])
    offset = lax.rem(me, GROUP // 2) * OWN
    own_source = lax.broadcasted_iota(jnp.int32, (width, 128), 0) - offset
    own_lane = lax.broadcasted_iota(jnp.int32, (width, 128), 1)
    own = exact_dot(picked, ((own_source == own_lane) & (own_lane < OWN)).astype(jnp.float32))
    loads[1].wait()
    relaxed = relax(
        tuple(short[i : i + 1, :] for i in range(3)), tuple(own[i : i + 1, :OWN] for i in range(4))
    )
    for i in range(3):
        stress[i : i + 1, :OWN] = relaxed[i]
    build_operators(wa, wb, wc)

    coord_c = coord(lax.broadcasted_iota(jnp.int32, (1, 1, LANES), 2) // PART)
    coord_all = coord(lax.broadcasted_iota(jnp.int32, (1, Q, 1), 1))


    def build_springs(index, carry):
        here = coord(index)
        squares = here * here + coord_all * coord_all + coord_c * coord_c
        spring[pl.ds(index, 1)] = 1.0 / (1.0 - squares / fene_limit)
        return carry

    lax.fori_loop(0, Q, build_springs, 0)

    def advance(part, last):
        k11, k12, k21, k22 = (lanes[part, i : i + 1, :].reshape(1, 1, LANES) for i in range(4))

        def first_direction(tile, carry):
            window = pl.ds(pl.multiple_of(tile * 8, 8), 8)
            value = grid[part, :, window, :]
            coord_a = coord(lax.broadcasted_iota(jnp.int32, (Q, 1, 1), 0))
            coord_b = coord(lax.broadcasted_iota(jnp.int32, (1, 8, 1), 1) + tile * 8)
            drift = (k11 - diffusion * spring[:, window, :]) * coord_a + k12 * coord_b
            moved = (drift * value).reshape(Q * 8, LANES)
            terms = jnp.concatenate(split(moved) + split(value.reshape(Q * 8, LANES)), axis=0)
            result = jnp.dot(wa[...], terms, preferred_element_type=jnp.float32)
            change[:, window, :] = result.reshape(Q, 8, LANES)
            return carry

        lax.fori_loop(0, 4, first_direction, 0)

        def other_directions(tile, carry):
            window = pl.ds(tile * 8, 8)
            value = grid[part, window]
            stiff = spring[window]
            coord_a = coord(lax.broadcasted_iota(jnp.int32, (8, 1, 1), 0) + tile * 8)
            pull = diffusion * stiff
            drift_b = k21 * coord_a + (k22 - pull) * coord_all
            moved_b = (drift_b * value).reshape(8 * Q, LANES)
            moved_c = (-pull * coord_c * value).reshape(8 * Q, LANES)
            plain = split(value.reshape(8 * Q, LANES))
            terms_b = jnp.concatenate(split(moved_b) + plain, axis=0)
            part_b = jnp.dot(wb[...], terms_b, preferred_element_type=jnp.float32)
            terms_c = jnp.concatenate(split(moved_c) + plain, axis=1)
            part_c = jnp.dot(terms_c, wc[...], preferred_element_type=jnp.float32)
            value = value + (change[window] + (part_b + part_c).reshape(8, Q, LANES))
            grid[part, window] = value
            if last:
                weighted = stiff * value
                sums[0] += jnp.sum(weighted, axis=0)
                weighted = weighted * coord_a
                sums[1] += jnp.sum(weighted, axis=0)
                sums[2] += jnp.sum(weighted * coord_a, axis=0)
                sums[3] += jnp.sum(value, axis=0)
            return carry

        lax.fori_loop(0, 4, other_directions, 0)

    def whole(part, carry):
        pltpu.make_async_copy(grid.at[part], grid.at[part], in_recv.at[part]).wait()
        sums[...] = jnp.zeros_like(sums)
        for turn in range(STEPS):
            advance(part, turn == STEPS - 1)

        def send_to(arrived, slot, place, turns):
            def send_out(turn, inner):
                target = peer(turn // 16, lax.rem(turn, 16))
                pltpu.make_async_remote_copy(
                    grid.at[part, target], arrived.at[place], out_send.at[part], out_recv.at[slot],
                    device_id={"conf": target}, device_id_type=MESH,
                ).start()
                return inner

            lax.fori_loop(*turns, send_out, 0)

        def keep(arrived, slot, place):
            pltpu.make_async_copy(grid.at[part, me], arrived.at[place], out_recv.at[slot]).start()

        @pl.when(part == 0)
        def _():
            send_to(early_back, 0, me, (1, GROUP))
            keep(early_back, 0, me)

        @pl.when(part == 1)
        def _():
            send_to(near_back, 1, lax.rem(me, 16), (1, 16))
            send_to(late, 2, lax.rem(me, 16), (16, GROUP))
            keep(near_back, 1, lax.rem(me, 16))

        column = coord(lax.broadcasted_iota(jnp.int32, (Q, 1), 0))
        scale = 1.0 / float(Q**3)
        stacked = jnp.concatenate(
            [
                jnp.sum(sums[2], axis=0, keepdims=True),
                jnp.sum(sums[1] * column, axis=0, keepdims=True),
                jnp.sum(sums[0] * (column * column), axis=0, keepdims=True),
                jnp.sum(sums[3], axis=0, keepdims=True),
                jnp.zeros((4, LANES), jnp.float32),
            ],
            axis=0,
        )
        fold_row = lax.broadcasted_iota(jnp.int32, (LANES, 128), 0) & (PART - 1)
        fold_lane = lax.broadcasted_iota(jnp.int32, (LANES, 128), 1) - my_c * PART
        moments[part] = exact_dot(stacked * scale, (fold_row == fold_lane).astype(jnp.float32))
        owner = part * (GROUP // 2) + me // 2

        @pl.when(owner != me)
        def _():
            pltpu.make_async_remote_copy(
                moments.at[part], inbox.at[my_c], note_send.at[part], note_recv.at[my_c],
                device_id={"conf": owner}, device_id_type=MESH,
            ).start()

        @pl.when(owner == me)
        def _():
            pltpu.make_async_copy(moments.at[part], inbox.at[my_c], note_recv.at[my_c]).start()

        return carry

    lax.fori_loop(0, PARTS, whole, 0)

    for i in range(2):
        pltpu.make_async_copy(inbox.at[i], inbox.at[i], note_recv.at[i]).wait()
    total = inbox[0] + inbox[1]
    for i, polymer in enumerate(
        (
            polymer_eta * (total[0:1] - total[3:4]),
            polymer_eta * total[1:2],
            polymer_eta * (total[2:3] - total[3:4]),
        )
    ):
        stress[i + 4 : i + 5, :OWN] = polymer[:, :OWN] + stress[i : i + 1, :OWN]

    pltpu.make_async_copy(early_back, early_back, out_recv.at[0]).wait()

    def early_side(block, carry):
        unpack(early_back, early.at[block], block)
        return carry

    lax.fori_loop(0, 2, early_side, 0)
    pltpu.make_async_copy(near_back, near_back, out_recv.at[1]).wait()
    unpack(near_back, early.at[2], 0)
    pltpu.make_async_copy(late, late, out_recv.at[2]).wait()
    others = pl.ds(0, GROUP - 1)
    for part in range(PARTS):
        pltpu.make_async_copy(packed.at[part, others], packed.at[part, others], in_send.at[part]).wait()
        pltpu.make_async_copy(grid.at[part, others], grid.at[part, others], out_send.at[part]).wait()

        @pl.when(part * (GROUP // 2) + me // 2 != me)
        def _(part=part):
            pltpu.make_async_copy(moments.at[part], moments.at[part], note_send.at[part]).wait()


def spread(early, late, stress, out_hbm, short_hbm, total_hbm, out, small, sem):
    near = lax.axis_index("conf") // 16
    columns = [0, 128] + [pl.multiple_of(place * 128, 128) for place in (2 + near, 3 - near)]
    copies = [
        pltpu.make_async_copy(early.at[i], out_hbm.at[:, pl.ds(columns[i], 128)], sem.at[i]) for i in range(3)
    ]
    for copy in copies:
        copy.start()
    for i, target in enumerate((short_hbm, total_hbm)):
        small[i] = stress[4 * i : 4 * i + 3, :OWN]
        copies.append(pltpu.make_async_copy(small.at[i], target, sem.at[3 + i]))
        copies[-1].start()
    unpack(late, out, 0)
    copies.append(pltpu.make_async_copy(out, out_hbm.at[:, pl.ds(columns[3], 128)], sem.at[5]))
    copies[-1].start()
    for copy in copies:
        copy.wait()


def on_device(density, velocity, short_stress):
    vmem = pl.BlockSpec(memory_space=pltpu.VMEM)
    hbm = pl.BlockSpec(memory_space=pltpu.HBM)
    blocks = (PARTS, GROUP, Q, LANES)
    dma = pltpu.SemaphoreType.DMA
    early, late, stress = pl.pallas_call(
        kernel,
        name="fokker_planck",
        out_shape=(
            jax.ShapeDtypeStruct((3, Q * Q, 128), jnp.float32),
            jax.ShapeDtypeStruct((GROUP // 2, Q, LANES), jnp.float32),
            jax.ShapeDtypeStruct((8, 128), jnp.float32),
        ),
        in_specs=[hbm] * 3,
        out_specs=(vmem, vmem, vmem),
        scratch_shapes=[
            pltpu.VMEM((4, Q * Q, 128), jnp.float32),
            pltpu.VMEM(velocity.shape, jnp.float32),
            pltpu.VMEM(short_stress.shape, jnp.float32),
            pltpu.VMEM((GROUP, Q, LANES), jnp.float32),
            pltpu.VMEM((GROUP // 2, Q, LANES), jnp.float32),
            pltpu.VMEM((2, 8, 128), jnp.float32),
            pltpu.VMEM(blocks, jnp.float32),
            pltpu.VMEM(blocks, jnp.float32),
            pltpu.VMEM((Q, Q, LANES), jnp.float32),
            pltpu.VMEM((Q, Q, LANES), jnp.float32),
            pltpu.VMEM((8 * Q, 6 * 8 * Q), jnp.bfloat16),
            pltpu.VMEM((8 * Q, 6 * 8 * Q), jnp.bfloat16),
            pltpu.VMEM((6 * LANES, LANES), jnp.bfloat16),
            pltpu.VMEM((2,) + velocity.shape, jnp.float32),
            pltpu.VMEM((PARTS, 8, LANES), jnp.float32),
            pltpu.VMEM((4, Q, LANES), jnp.float32),
            pltpu.VMEM((PARTS, 8, 128), jnp.float32),
            dma((PARTS,)),
            dma((PARTS,)),
            dma((PARTS,)),
            dma((PARTS + 1,)),
            dma((2,)),
            dma((2,)),
            dma((2,)),
            dma((4,)),
            dma((PARTS,)),
            dma((2,)),
        ],
        compiler_params=pltpu.CompilerParams(
            collective_id=0, has_side_effects=True, vmem_limit_bytes=VMEM_LIMIT
        ),
    )(
        *(
            pltpu.with_memory_space_constraint(one, pltpu.HBM)
            for one in (density.reshape(Q * Q, CELLS), velocity, short_stress)
        ),
    )
    result, short_next, total_stress = pl.pallas_call(
        spread,
        name="spread",
        out_shape=(
            jax.ShapeDtypeStruct((Q * Q, CELLS), jnp.float32),
            jax.ShapeDtypeStruct(short_stress.shape, jnp.float32),
            jax.ShapeDtypeStruct(short_stress.shape, jnp.float32),
        ),
        in_specs=[vmem, vmem, vmem],
        out_specs=(hbm, hbm, hbm),
        scratch_shapes=[
            pltpu.VMEM((Q * Q, 128), jnp.float32),
            pltpu.VMEM((2,) + short_stress.shape, jnp.float32),
            dma((6,)),
        ],
        compiler_params=pltpu.CompilerParams(vmem_limit_bytes=VMEM_LIMIT),
    )(early, late, stress)
    return result.reshape(density.shape), short_next, total_stress


def solution(mesh):
    return jax.shard_map(
        on_device,
        mesh=mesh,
        in_specs=(P("conf", None, None, "cell"), P(None, "cell", None), P(None, ("cell", "conf"))),
        out_specs=(
            P("conf", None, None, "cell"),
            P(None, ("cell", "conf")),
            P(None, ("cell", "conf")),
        ),
        check_vma=False,
    )
```

```python
import functools

import jax
import jax.numpy as jnp
import numpy as np
from jax import lax
from jax.experimental import pallas as pl
from jax.experimental.pallas import tpu as pltpu
from jax.sharding import PartitionSpec as P

STEPS = 2
half_extent = 3.0
fene_limit = 50.0
diffusion = 0.5
time_step = 0.001
polymer_eta = 1.0
solvent_eta = 0.5
short_relax = 0.01

MESH = pl.DeviceIdType.MESH
Q = 32
GROUP = 32
OWN = 16
PART = 8
PARTS = 2
LANES = Q * PART
CELLS = GROUP * OWN
TALL = 32
VMEM_LIMIT = 50 * 1024 * 1024


def stencils():
    offsets = np.arange(Q)[:, None] - np.arange(Q)[None, :]
    angle = offsets * (np.pi / Q)
    sine = np.where(offsets == 0, 1.0, np.sin(angle))
    first = np.where(offsets % 2 == 0, 1.0, -1.0) * np.cos(angle) / sine * (np.pi / (2 * half_extent))
    first = np.where(offsets == 0, 0.0, first)
    return (-time_step * first)[:, 0], (time_step * diffusion * (first @ first))[:, 0]


def build_operators(wa, wb, wc):
    first, second = stencils()
    size = 8 * Q
    row = lax.broadcasted_iota(jnp.int32, (size, size), 0)
    column = lax.broadcasted_iota(jnp.int32, (size, size), 1)

    def circulant(offset, inside):
        key = jnp.where(inside, offset & (Q - 1), -1)
        one, two = (jnp.zeros((size, size), jnp.float32) for _ in range(2))
        for i in range(Q):
            here = key == i
            one = jnp.where(here, jnp.float32(first[i]), one)
            two = jnp.where(here, jnp.float32(second[i]), two)
        return one, two

    def store(ref, matrix, at, by_row):
        high, low, again = split(matrix)
        for i, value in enumerate((high, again, low)):
            place = pl.ds((at + i) * size, size)
            if by_row:
                ref[place, :] = value
            else:
                ref[:, place] = value

    one, two = circulant((row >> 3) - (column >> 3), (row & 7) == (column & 7))
    store(wa, one, 0, False)
    store(wa, two, 3, False)
    store(wc, -one, 0, True)
    store(wc, two, 3, True)
    one, two = circulant(row - column, (row >> 5) == (column >> 5))
    store(wb, one, 0, False)
    store(wb, two, 3, False)


def coord(index):
    return -half_extent + (index.astype(jnp.float32) + 0.5) * (2.0 * half_extent / Q)


def split(value):
    high = value.astype(jnp.bfloat16)
    low = (value - high.astype(jnp.float32)).astype(jnp.bfloat16)
    return [high, low, high]


def exchange_lanes(values):
    lane = lax.broadcasted_iota(jnp.int32, values[0].shape, 1)
    values = list(values)
    for bit in (1, 2, 4, 8):
        upper = (lane & (8 * bit)) != 0
        shift = 8 * bit
        for i in range(16):
            if i & bit:
                continue
            one, two = values[i], values[i | bit]
            mixed = jnp.where(upper, one, two)
            if shift == 64:
                mixed = pltpu.roll(mixed, 64, 1)
            else:
                mixed = jnp.take_along_axis(mixed, lane ^ shift, axis=1, mode="promise_in_bounds")
            values[i] = jnp.where(upper, mixed, one)
            values[i | bit] = jnp.where(upper, two, mixed)
    return values


def unpack(arrived, target, block, tall=TALL, first=0, last=2 * Q // TALL):
    def piece(turn, carry):
        tile, half = turn // 2, turn % 2
        values = [
            arrived[
                block * 16 + i, pl.ds(tile * tall, tall),
                pl.ds(half * 128, 128),
            ]
            for i in range(16)
        ]
        values = exchange_lanes(values)
        for i in range(16):
            target[pl.ds(tile * (tall * Q) + half * 16 + i, tall, stride=Q), :] = values[i]
        return carry

    for turn in range(first, last):
        piece(turn, 0)


def exact_dot(one, two):
    return jnp.dot(one, two, precision=lax.Precision.HIGHEST, preferred_element_type=jnp.float32)


def relax(stress, gradient):
    stress_xx, stress_xy, stress_yy = stress
    for _ in range(STEPS):
        next_xx = stress_xx + time_step * (
            2.0 * (gradient[0] * stress_xx + gradient[1] * stress_xy)
            - (stress_xx - 2.0 * solvent_eta * gradient[0]) / short_relax
        )
        next_xy = stress_xy + time_step * (
            gradient[0] * stress_xy
            + gradient[1] * stress_yy
            + gradient[2] * stress_xx
            + gradient[3] * stress_xy
            - (stress_xy - solvent_eta * (gradient[1] + gradient[2])) / short_relax
        )
        next_yy = stress_yy + time_step * (
            2.0 * (gradient[2] * stress_xy + gradient[3] * stress_yy)
            - (stress_yy - 2.0 * solvent_eta * gradient[3]) / short_relax
        )
        stress_xx, stress_xy, stress_yy = next_xx, next_xy, next_yy
    return stress_xx, stress_xy, stress_yy


def kernel(
    density_hbm, velocity_hbm, short_hbm,
    early, late, stress,
    density, velocity, short, early_back, near_back, inbox, packed, grid, change, spring, wa, wb, wc, halo, lanes, sums, moments,
    in_send, in_recv, out_send, out_recv, load_sem, halo_send, halo_recv, read_sem,
    note_send, note_recv,
):
    me = lax.axis_index("conf")
    my_y, my_z, my_c = me // 8, (me // 2) % 4, me % 2
    brick = lax.axis_index("cell")
    bricks = lax.axis_size("cell")
    above, below = lax.rem(brick + bricks - 1, bricks), lax.rem(brick + 1, bricks)

    reads = [
        pltpu.make_async_copy(
            density_hbm.at[:, pl.ds(pl.multiple_of(block * 128, 128), 128)], density.at[block], read_sem.at[i]
        )
        for i, block in enumerate([2 * (i // 2) + lax.rem(my_y // 2 + i, 2) for i in range(4)])
    ]
    reads[0].start()
    barrier = pltpu.get_barrier_semaphore()

    for turn in sorted(range(1, GROUP), key=lambda turn: -(turn // 2 % 4 == 2) - (turn // 2 % 4 > 0)):
        pl.semaphore_signal(
            barrier, inc=1,
            device_id={"conf": lax.rem(my_y + turn // 8, 4) * 8 + lax.rem(my_z + turn // 2, 4) * 2 + lax.rem(my_c + turn, 2)},
            device_id_type=MESH,
        )
    for other in (above, below):
        pl.semaphore_signal(barrier, inc=1, device_id={"cell": other}, device_id_type=MESH)

    for read in reads[1:]:
        read.start()
    loads = [
        pltpu.make_async_copy(source, target, load_sem.at[i])
        for i, (source, target) in enumerate(
            ((velocity_hbm, velocity), (short_hbm, short))
        )
    ]
    for load in loads:
        load.start()

    def side(turn):
        return lax.rem(my_y // 2 + turn, 2)

    def peer(half, turn):
        y = 2 * side(half) + lax.rem(my_y + turn // 8, 2)
        z = lax.rem(my_z + lax.rem(turn, 8) // 2, 4)
        return y * 8 + z * 2 + lax.rem(my_c + turn, 2)

    def pack(part, half):
        first = side(half)
        block = part * 2 + first

        def piece(turn, carry):
            tile, half = turn // 2, turn % 2
            values = [
                density[block, pl.ds(tile * (TALL * Q) + half * 16 + i, TALL, stride=Q), :] for i in range(16)
            ]
            values = exchange_lanes(values)
            for i in range(16):
                packed[
                    part, first * 16 + i, pl.ds(tile * TALL, TALL),
                    pl.ds(half * 128, 128),
                ] = values[i]
            return carry

        for turn in range(2 * Q // TALL):
            piece(turn, 0)

    def send_in(part, half):
        def one(turn, carry):
            target = peer(half, turn)
            pltpu.make_async_remote_copy(
                packed.at[part, target], grid.at[part, me], in_send.at[part], in_recv.at[part],
                device_id={"conf": target}, device_id_type=MESH,
            ).start()
            return carry

        for turn in range(1 if half == 0 else 0, 16):
            one(turn, 0)

    reads[0].wait()
    pack(0, 0)
    pl.semaphore_wait(barrier, GROUP + 1)
    send_in(0, 0)
    loads[0].wait()
    to_above = pltpu.make_async_remote_copy(
        velocity, halo.at[1], halo_send.at[0], halo_recv.at[1], device_id={"cell": above}, device_id_type=MESH
    )
    to_below = pltpu.make_async_remote_copy(
        velocity, halo.at[0], halo_send.at[1], halo_recv.at[0], device_id={"cell": below}, device_id_type=MESH
    )
    to_above.start()
    to_below.start()
    for i in range(1, 4):
        reads[i].wait()
        pack(i // 2, i % 2)
        send_in(i // 2, i % 2)
    for part in range(PARTS):
        pltpu.make_async_copy(packed.at[part, me], grid.at[part, me], in_recv.at[part]).start()

    to_above.wait()
    to_below.wait()
    last_row = velocity.shape[1] - 1
    gradients = [[], []]
    for i in range(2):
        here = velocity[i]
        along = (pltpu.roll(here, here.shape[1] - 1, 1) - pltpu.roll(here, 1, 1)) * 0.5
        down = (
            (here[1:2] - halo[0, i][last_row : last_row + 1]) * 0.5,
            (halo[1, i][0:1] - here[0:1]) * 0.5,
        )
        for part in range(PARTS):
            gradients[part] += [along[part : part + 1], down[part]]
    width = velocity.shape[2]
    filler = [jnp.zeros((4, width), jnp.float32)]
    gradients = [jnp.concatenate(one + filler, axis=0) for one in gradients]
    source = lax.broadcasted_iota(jnp.int32, (width, LANES), 0) - me * PART
    lane = lax.broadcasted_iota(jnp.int32, (width, LANES), 1)
    choose = (source == (lane & (PART - 1))).astype(jnp.float32)
    for part in range(PARTS):
        lanes[part] = exact_dot(gradients[part], choose)
    picked = jnp.where(me < GROUP // 2, gradients[0], gradients[1])
    offset = lax.rem(me, GROUP // 2) * OWN
    own_source = lax.broadcasted_iota(jnp.int32, (width, 128), 0) - offset
    own_lane = lax.broadcasted_iota(jnp.int32, (width, 128), 1)
    own = exact_dot(picked, ((own_source == own_lane) & (own_lane < OWN)).astype(jnp.float32))
    loads[1].wait()
    relaxed = relax(
        tuple(short[i : i + 1, :] for i in range(3)), tuple(own[i : i + 1, :OWN] for i in range(4))
    )
    for i in range(3):
        stress[i : i + 1, :OWN] = relaxed[i]
    build_operators(wa, wb, wc)

    coord_c = coord(lax.broadcasted_iota(jnp.int32, (1, 1, LANES), 2) // PART)
    coord_all = coord(lax.broadcasted_iota(jnp.int32, (1, Q, 1), 1))


    def build_springs(index, carry):
        here = coord(index)
        squares = here * here + coord_all * coord_all + coord_c * coord_c
        spring[pl.ds(index, 1)] = 1.0 / (1.0 - squares / fene_limit)
        return carry

    lax.fori_loop(0, Q, build_springs, 0)

    def advance(part, last):
        k11, k12, k21, k22 = (lanes[part, i : i + 1, :].reshape(1, 1, LANES) for i in range(4))

        def first_direction(tile, carry):
            window = pl.ds(pl.multiple_of(tile * 8, 8), 8)
            value = grid[part, :, window, :]
            coord_a = coord(lax.broadcasted_iota(jnp.int32, (Q, 1, 1), 0))
            coord_b = coord(lax.broadcasted_iota(jnp.int32, (1, 8, 1), 1) + tile * 8)
            drift = (k11 - diffusion * spring[:, window, :]) * coord_a + k12 * coord_b
            moved = (drift * value).reshape(Q * 8, LANES)
            terms = jnp.concatenate(split(moved) + split(value.reshape(Q * 8, LANES)), axis=0)
            result = jnp.dot(wa[...], terms, preferred_element_type=jnp.float32)
            change[:, window, :] = result.reshape(Q, 8, LANES)
            return carry

        lax.fori_loop(0, 4, first_direction, 0)

        def other_directions(tile, carry):
            window = pl.ds(tile * 8, 8)
            value = grid[part, window]
            stiff = spring[window]
            coord_a = coord(lax.broadcasted_iota(jnp.int32, (8, 1, 1), 0) + tile * 8)
            pull = diffusion * stiff
            drift_b = k21 * coord_a + (k22 - pull) * coord_all
            moved_b = (drift_b * value).reshape(8 * Q, LANES)
            moved_c = (-pull * coord_c * value).reshape(8 * Q, LANES)
            plain = split(value.reshape(8 * Q, LANES))
            terms_b = jnp.concatenate(split(moved_b) + plain, axis=0)
            part_b = jnp.dot(wb[...], terms_b, preferred_element_type=jnp.float32)
            terms_c = jnp.concatenate(split(moved_c) + plain, axis=1)
            part_c = jnp.dot(terms_c, wc[...], preferred_element_type=jnp.float32)
            value = value + (change[window] + (part_b + part_c).reshape(8, Q, LANES))
            grid[part, window] = value
            if last:
                weighted = stiff * value
                sums[0] += jnp.sum(weighted, axis=0)
                weighted = weighted * coord_a
                sums[1] += jnp.sum(weighted, axis=0)
                sums[2] += jnp.sum(weighted * coord_a, axis=0)
                sums[3] += jnp.sum(value, axis=0)
            return carry

        lax.fori_loop(0, 4, other_directions, 0)

    def whole(part, carry):
        pltpu.make_async_copy(grid.at[part], grid.at[part], in_recv.at[part]).wait()
        sums[...] = jnp.zeros_like(sums)
        for turn in range(STEPS):
            advance(part, turn == STEPS - 1)

        def send_to(arrived, slot, place, turns):
            def send_out(turn, inner):
                target = peer(turn // 16, lax.rem(turn, 16))
                pltpu.make_async_remote_copy(
                    grid.at[part, target], arrived.at[place], out_send.at[part], out_recv.at[slot],
                    device_id={"conf": target}, device_id_type=MESH,
                ).start()
                return inner

            lax.fori_loop(*turns, send_out, 0)

        def keep(arrived, slot, place):
            pltpu.make_async_copy(grid.at[part, me], arrived.at[place], out_recv.at[slot]).start()

        @pl.when(part == 0)
        def _():
            send_to(early_back, 0, me, (1, GROUP))
            keep(early_back, 0, me)

        @pl.when(part == 1)
        def _():
            send_to(near_back, 1, lax.rem(me, 16), (1, 16))
            send_to(late, 2, lax.rem(me, 16), (16, GROUP))
            keep(near_back, 1, lax.rem(me, 16))

        column = coord(lax.broadcasted_iota(jnp.int32, (Q, 1), 0))
        scale = 1.0 / float(Q**3)
        stacked = jnp.concatenate(
            [
                jnp.sum(sums[2], axis=0, keepdims=True),
                jnp.sum(sums[1] * column, axis=0, keepdims=True),
                jnp.sum(sums[0] * (column * column), axis=0, keepdims=True),
                jnp.sum(sums[3], axis=0, keepdims=True),
                jnp.zeros((4, LANES), jnp.float32),
            ],
            axis=0,
        )
        fold_row = lax.broadcasted_iota(jnp.int32, (LANES, 128), 0) & (PART - 1)
        fold_lane = lax.broadcasted_iota(jnp.int32, (LANES, 128), 1) - my_c * PART
        moments[part] = exact_dot(stacked * scale, (fold_row == fold_lane).astype(jnp.float32))
        owner = part * (GROUP // 2) + me // 2

        @pl.when(owner != me)
        def _():
            pltpu.make_async_remote_copy(
                moments.at[part], inbox.at[my_c], note_send.at[part], note_recv.at[my_c],
                device_id={"conf": owner}, device_id_type=MESH,
            ).start()

        @pl.when(owner == me)
        def _():
            pltpu.make_async_copy(moments.at[part], inbox.at[my_c], note_recv.at[my_c]).start()

        return carry

    lax.fori_loop(0, PARTS, whole, 0)

    for i in range(2):
        pltpu.make_async_copy(inbox.at[i], inbox.at[i], note_recv.at[i]).wait()
    total = inbox[0] + inbox[1]
    for i, polymer in enumerate(
        (
            polymer_eta * (total[0:1] - total[3:4]),
            polymer_eta * total[1:2],
            polymer_eta * (total[2:3] - total[3:4]),
        )
    ):
        stress[i + 4 : i + 5, :OWN] = polymer[:, :OWN] + stress[i : i + 1, :OWN]

    pltpu.make_async_copy(early_back, early_back, out_recv.at[0]).wait()

    def early_side(block, carry):
        unpack(early_back, early.at[block], block)
        return carry

    lax.fori_loop(0, 2, early_side, 0)
    pltpu.make_async_copy(near_back, near_back, out_recv.at[1]).wait()
    unpack(near_back, early.at[2], 0)
    pltpu.make_async_copy(late, late, out_recv.at[2]).wait()
    others = pl.ds(0, GROUP - 1)
    for part in range(PARTS):
        pltpu.make_async_copy(packed.at[part, others], packed.at[part, others], in_send.at[part]).wait()
        pltpu.make_async_copy(grid.at[part, others], grid.at[part, others], out_send.at[part]).wait()

        @pl.when(part * (GROUP // 2) + me // 2 != me)
        def _(part=part):
            pltpu.make_async_copy(moments.at[part], moments.at[part], note_send.at[part]).wait()


def spread(early, late, stress, out_hbm, short_hbm, total_hbm, out, small, sem):
    near = lax.axis_index("conf") // 16
    columns = [0, 128] + [pl.multiple_of(place * 128, 128) for place in (2 + near, 3 - near)]
    copies = [
        pltpu.make_async_copy(early.at[i], out_hbm.at[:, pl.ds(columns[i], 128)], sem.at[i]) for i in range(3)
    ]
    for copy in copies:
        copy.start()
    for i, target in enumerate((short_hbm, total_hbm)):
        small[i] = stress[4 * i : 4 * i + 3, :OWN]
        copies.append(pltpu.make_async_copy(small.at[i], target, sem.at[3 + i]))
        copies[-1].start()
    for i in range(2):
        unpack(late, out, 0, Q // 2, 2 * i, 2 * i + 2)
        rows = pl.ds(i * (Q * Q // 2), Q * Q // 2)
        copies.append(pltpu.make_async_copy(out.at[rows], out_hbm.at[rows, pl.ds(columns[3], 128)], sem.at[5 + i]))
        copies[-1].start()
    for copy in copies:
        copy.wait()


def on_device(density, velocity, short_stress):
    vmem = pl.BlockSpec(memory_space=pltpu.VMEM)
    hbm = pl.BlockSpec(memory_space=pltpu.HBM)
    blocks = (PARTS, GROUP, Q, LANES)
    dma = pltpu.SemaphoreType.DMA
    early, late, stress = pl.pallas_call(
        kernel,
        name="fokker_planck",
        out_shape=(
            jax.ShapeDtypeStruct((3, Q * Q, 128), jnp.float32),
            jax.ShapeDtypeStruct((GROUP // 2, Q, LANES), jnp.float32),
            jax.ShapeDtypeStruct((8, 128), jnp.float32),
        ),
        in_specs=[hbm] * 3,
        out_specs=(vmem, vmem, vmem),
        scratch_shapes=[
            pltpu.VMEM((4, Q * Q, 128), jnp.float32),
            pltpu.VMEM(velocity.shape, jnp.float32),
            pltpu.VMEM(short_stress.shape, jnp.float32),
            pltpu.VMEM((GROUP, Q, LANES), jnp.float32),
            pltpu.VMEM((GROUP // 2, Q, LANES), jnp.float32),
            pltpu.VMEM((2, 8, 128), jnp.float32),
            pltpu.VMEM(blocks, jnp.float32),
            pltpu.VMEM(blocks, jnp.float32),
            pltpu.VMEM((Q, Q, LANES), jnp.float32),
            pltpu.VMEM((Q, Q, LANES), jnp.float32),
            pltpu.VMEM((8 * Q, 6 * 8 * Q), jnp.bfloat16),
            pltpu.VMEM((8 * Q, 6 * 8 * Q), jnp.bfloat16),
            pltpu.VMEM((6 * LANES, LANES), jnp.bfloat16),
            pltpu.VMEM((2,) + velocity.shape, jnp.float32),
            pltpu.VMEM((PARTS, 8, LANES), jnp.float32),
            pltpu.VMEM((4, Q, LANES), jnp.float32),
            pltpu.VMEM((PARTS, 8, 128), jnp.float32),
            dma((PARTS,)),
            dma((PARTS,)),
            dma((PARTS,)),
            dma((PARTS + 1,)),
            dma((2,)),
            dma((2,)),
            dma((2,)),
            dma((4,)),
            dma((PARTS,)),
            dma((2,)),
        ],
        compiler_params=pltpu.CompilerParams(
            collective_id=0, has_side_effects=True, vmem_limit_bytes=VMEM_LIMIT
        ),
    )(
        *(
            pltpu.with_memory_space_constraint(one, pltpu.HBM)
            for one in (density.reshape(Q * Q, CELLS), velocity, short_stress)
        ),
    )
    result, short_next, total_stress = pl.pallas_call(
        spread,
        name="spread",
        out_shape=(
            jax.ShapeDtypeStruct((Q * Q, CELLS), jnp.float32),
            jax.ShapeDtypeStruct(short_stress.shape, jnp.float32),
            jax.ShapeDtypeStruct(short_stress.shape, jnp.float32),
        ),
        in_specs=[vmem, vmem, vmem],
        out_specs=(hbm, hbm, hbm),
        scratch_shapes=[
            pltpu.VMEM((Q * Q, 128), jnp.float32),
            pltpu.VMEM((2,) + short_stress.shape, jnp.float32),
            dma((7,)),
        ],
        compiler_params=pltpu.CompilerParams(vmem_limit_bytes=VMEM_LIMIT),
    )(early, late, stress)
    return result.reshape(density.shape), short_next, total_stress


def solution(mesh):
    return jax.shard_map(
        on_device,
        mesh=mesh,
        in_specs=(P("conf", None, None, "cell"), P(None, "cell", None), P(None, ("cell", "conf"))),
        out_specs=(
            P("conf", None, None, "cell"),
            P(None, ("cell", "conf")),
            P(None, ("cell", "conf")),
        ),
        check_vma=False,
    )
```
